32 devices in a mesh: dp: 8 (over z, core), ctx: 4 (over y, x).
Axes of the slice: x: 2, y: 2, z: 4, core: 2. Of those that a mesh axis runs over, the one named last changes fastest.
Arguments:
- inputs: bfloat16 [8, 4, 256, 2048], P('dp', 'ctx'), may hold values from -6 to 6
- positions: int32 [8, 4, 256], P('dp', 'ctx'), may hold values from 0 to 3071, as said below
- block_order: int32 [4, 2], replicated, may hold values from 0 to 7, as said below
- norm_attn: bfloat16 [2048], P(('dp', 'ctx')), may hold values from 0.099609375 to 1.8984375
- w_query: bfloat16 [2048, 2048], P(('dp', 'ctx')), may hold values from -0.125 to 0.125
- w_key: bfloat16 [2048, 256], P(('dp', 'ctx')), may hold values from -0.125 to 0.125
- w_value: bfloat16 [2048, 256], P(('dp', 'ctx')), may hold values from -0.125 to 0.125
- w_out: bfloat16 [2048, 2048], P(('dp', 'ctx')), may hold values from -1 to 1
- norm_mlp: bfloat16 [2048], P(('dp', 'ctx')), may hold values from 0.099609375 to 1.8984375
- w_gate: bfloat16 [2048, 5632], P(('dp', 'ctx')), may hold values from -0.125 to 0.125
- w_up: bfloat16 [2048, 5632], P(('dp', 'ctx')), may hold values from -0.125 to 0.125
- w_down: bfloat16 [5632, 2048], P(('dp', 'ctx')), may hold values from -0.078125 to 0.078125
- cotangent: bfloat16 [8, 4, 256, 2048], P('dp', 'ctx'), may hold values from -6 to 6
Outputs:
- outputs: bfloat16 [8, 4, 256, 2048], P('dp', 'ctx')
- grad_inputs: float32 [8, 4, 256, 2048], P('dp', 'ctx')
- grad_norm_attn: float32 [2048], P(('dp', 'ctx'))
- grad_w_query: float32 [2048, 2048], P(('dp', 'ctx'))
- grad_w_key: float32 [2048, 256], P(('dp', 'ctx'))
- grad_w_value: float32 [2048, 256], P(('dp', 'ctx'))
- grad_w_out: float32 [2048, 2048], P(('dp', 'ctx'))
- grad_norm_mlp: float32 [2048], P(('dp', 'ctx'))
- grad_w_gate: float32 [2048, 5632], P(('dp', 'ctx'))
- grad_w_up: float32 [2048, 5632], P(('dp', 'ctx'))
- grad_w_down: float32 [5632, 2048], P(('dp', 'ctx'))
The draws below stay inside these ranges and needn't reach their ends.
Inputs may be any that keep to these rules, and one draw needn't show every extreme that they name: `block_order`: each row of the table is one context rank's two logical blocks of 128 tokens, in the order its rows hold them; every block number appears exactly once. Within a sequence the positions rise strictly along the logical token order; its logical first token has position 0 and its last 3071.
All inputs are finite; a program needn't handle non-finite values.
Results may differ from the reference program's by a relative error of at most 0.029.
Values may be sent and summed in bfloat16 or wider, within the bound.
No kernel may reach another device: no remote copies, remote signals or barrier semaphores. Data moves between devices by JAX's collectives and lax.ppermute only.
A program may use at most 384 MiB of HBM per device.

```python
import jax
import jax.numpy as jnp
from jax import lax

D = 2048
HEADS = 32
KV_HEADS = 4
HEAD_DIM = 64
FF = 5632
TOK_DEV = 256
QW = 2048
KVW = 256
BLOCK = 128
SEQ_LEN = 1024
SEQS = 8
N_CTX = 4


def order_table(key):
    picked = jax.random.permutation(jax.random.fold_in(key, 17), 2 * N_CTX)
    return picked.astype(jnp.int32).reshape(N_CTX, 2)


def draw_block_order(key, part):
    table = order_table(key)
    return table


def draw_positions(key, part):
    table = order_table(key)
    key = jax.random.fold_in(key, 2)
    increments = jax.random.randint(key, (SEQS, SEQ_LEN), 1, 4, dtype=jnp.int32)
    climbed = jnp.cumsum(increments, 1) - increments[:, :1]
    climbed = climbed.at[:, SEQ_LEN - 1].set(3 * SEQ_LEN - 1)
    offsets = jnp.arange(BLOCK, dtype=jnp.int32)
    lookup = (table[:, :, None] * BLOCK + offsets[None, None, :]).reshape(N_CTX, TOK_DEV)
    return climbed[:, lookup].astype(jnp.int32)


def steps_of(stream_key, dims, cuts, least, high):
    loudness, own = 1.0, jax.random.fold_in(stream_key, 6)
    for dim, shards_of in cuts:
        draws = jnp.exp(jax.random.uniform(jax.random.fold_in(own, dim), (shards_of,), jnp.float32, least / len(cuts), high / len(cuts)))
        loudness = loudness * jnp.repeat(draws, dims[dim] // shards_of).reshape([-1 if axis == dim else 1 for axis in range(len(dims))])
    return loudness


def scatter_about(key, dims, width, limit, cuts=(), kind=jnp.bfloat16):
    entries = width * jax.random.normal(key, dims, jnp.float32)
    if cuts:
        entries = entries * steps_of(key, dims, cuts, -0.22, 0.18)
    return jnp.clip(entries, -limit, limit).astype(kind)


def setup_inputs(seed: int = 0) -> dict:
    streams_of = jax.random.split(jax.random.key(seed), 14)
    return {
        "inputs": scatter_about(streams_of[0], (SEQS, N_CTX, TOK_DEV, D), 1.0, 6.0, ((0, 8), (1, 4))),
        "positions": draw_positions(jax.random.fold_in(streams_of[13], 71), 0),
        "block_order": draw_block_order(jax.random.fold_in(streams_of[13], 71), 0),
        "norm_attn": jnp.clip(1.0 + 0.18 * jax.random.normal(streams_of[3], (D,), jnp.float32), 0.099609375, 1.8984375).astype(jnp.bfloat16),
        "w_query": scatter_about(streams_of[4], (D, QW), D ** -0.5, 0.125, ((0, 32),)),
        "w_key": scatter_about(streams_of[5], (D, KVW), D ** -0.5, 0.125, ((0, 32),)),
        "w_value": scatter_about(streams_of[6], (D, KVW), D ** -0.5, 0.125, ((0, 32),)),
        "w_out": scatter_about(streams_of[7], (QW, D), (QW // 64) ** -0.5, 1.0, ((0, 32),)),
        "norm_mlp": jnp.clip(1.0 + 0.18 * jax.random.normal(streams_of[8], (D,), jnp.float32), 0.099609375, 1.8984375).astype(jnp.bfloat16),
        "w_gate": scatter_about(streams_of[9], (D, FF), D ** -0.5, 0.125, ((0, 32),)),
        "w_up": scatter_about(streams_of[10], (D, FF), D ** -0.5, 0.125, ((0, 32),)),
        "w_down": scatter_about(streams_of[11], (FF, D), FF ** -0.5, 0.078125, ((0, 32),)),
        "cotangent": scatter_about(streams_of[12], (SEQS, N_CTX, TOK_DEV, D), 1.0, 6.0, ((0, 8), (1, 4))),
    }


NORM_EPS = 1e-05
ROPE_BASE = 10000.0
MASKED_SCORE = -1e+30
HIGHEST = lax.Precision.HIGHEST

@jax.custom_vjp
def low(v):
    return lax.optimization_barrier(v.astype(jnp.bfloat16)).astype(jnp.float32)

@jax.custom_vjp
def low_back(v):
    return v

def low_keep(v):
    return (low(v), None)

def low_pass(kept, grad):
    return (grad,)

def back_keep(v):
    return (v, None)

def back_low(kept, grad):
    return (low(grad),)
low.defvjp(low_keep, low_pass)
low_back.defvjp(back_keep, back_low)

def matmul(left, right):
    return jnp.dot(left, right, preferred_element_type=jnp.float32, precision=HIGHEST)

def rotate(values, angles):
    cosine = jnp.cos(angles)
    sine = jnp.sin(angles)
    cosine = jnp.concatenate([cosine, cosine], -1)[:, None, :]
    sine = jnp.concatenate([sine, sine], -1)[:, None, :]
    half_dim = values.shape[-1] // 2
    turned = jnp.concatenate([-values[..., half_dim:], values[..., :half_dim]], -1)
    return values * cosine + turned * sine

def layer(seq_rows, angles, logical, weights):
    norm_attn, w_query, w_key, w_value, w_out, norm_mlp, w_gate, w_up, w_down = weights
    length = seq_rows.shape[0]
    group_size = HEADS // KV_HEADS
    scale_attn = lax.rsqrt(lax.optimization_barrier(jnp.mean(seq_rows * seq_rows, -1, keepdims=True)) + NORM_EPS)
    hidden_attn = low(seq_rows * scale_attn * norm_attn)
    queries = low_back(matmul(hidden_attn, w_query)).reshape(length, HEADS, HEAD_DIM)
    queries = low(rotate(queries, angles)).reshape(length, KV_HEADS, group_size, HEAD_DIM)
    key_heads = low_back(matmul(hidden_attn, w_key)).reshape(length, KV_HEADS, HEAD_DIM)
    key_heads = low(rotate(key_heads, angles))
    value_heads = low(low_back(matmul(hidden_attn, w_value))).reshape(length, KV_HEADS, HEAD_DIM)

    def attend(first_row):
        query_block = lax.dynamic_slice_in_dim(queries, first_row, TOK_DEV, 0)
        query_index = lax.dynamic_slice_in_dim(logical, first_row, TOK_DEV, 0)
        scores = jnp.einsum('qgjd,kgd->gjqk', query_block, key_heads, precision=HIGHEST) * HEAD_DIM ** (-0.5)
        scores = low_back(scores)
        visible = logical[None, :] <= query_index[:, None]
        scores = jnp.where(visible, scores, MASKED_SCORE)
        top_score = lax.optimization_barrier(jnp.max(scores, -1, keepdims=True))
        exp_scores = jnp.exp(scores - top_score)
        probabilities = exp_scores / lax.optimization_barrier(jnp.sum(exp_scores, -1, keepdims=True))
        mixture = jnp.einsum('gjqk,kgd->qgjd', low(probabilities), value_heads, precision=HIGHEST)
        return mixture.reshape(TOK_DEV, QW)
    block_starts = jnp.arange(N_CTX, dtype=jnp.int32) * TOK_DEV
    attended = lax.map(jax.checkpoint(attend), block_starts).reshape(length, QW)
    attended = low(low_back(attended))
    middle = seq_rows + low_back(matmul(attended, w_out))
    scale_mlp = lax.rsqrt(lax.optimization_barrier(jnp.mean(middle * middle, -1, keepdims=True)) + NORM_EPS)
    hidden_mlp = low(middle * scale_mlp * norm_mlp)
    gate_rows = low_back(matmul(hidden_mlp, w_gate))
    up_rows = low_back(matmul(hidden_mlp, w_up))
    activated = low(gate_rows * jax.nn.sigmoid(gate_rows) * up_rows)
    return middle + low_back(matmul(activated, w_down))

def reference(inputs, positions, block_order, norm_attn, w_query, w_key, w_value, w_out, norm_mlp, w_gate, w_up, w_down, cotangent):
    weights = tuple((tensor.astype(jnp.float32) for tensor in (norm_attn, w_query, w_key, w_value, w_out, norm_mlp, w_gate, w_up, w_down)))
    seq_inputs = inputs.reshape(SEQS, SEQ_LEN, D).astype(jnp.float32)
    seq_grads = cotangent.reshape(SEQS, SEQ_LEN, D).astype(jnp.float32)
    seq_positions = positions.reshape(SEQS, SEQ_LEN)
    row_index = jnp.arange(SEQ_LEN, dtype=jnp.int32)
    logical = block_order.reshape(-1)[row_index // BLOCK] * BLOCK + row_index % BLOCK
    frequency = ROPE_BASE ** (-jnp.arange(HEAD_DIM // 2, dtype=jnp.float32) * 2.0 / HEAD_DIM)

    def one_sequence(totals, pieces):
        seq_rows, seq_pos, seq_grad = pieces
        angles = seq_pos.astype(jnp.float32)[:, None] * frequency[None, :]

        def forward(rows_in, params):
            return layer(rows_in, angles, logical, params)
        result, pullback = jax.vjp(forward, seq_rows, weights)
        grad_rows, grad_params = pullback(seq_grad)
        totals = jax.tree.map(jnp.add, totals, grad_params)
        return (totals, (result.astype(jnp.bfloat16), grad_rows))
    start_totals = jax.tree.map(jnp.zeros_like, weights)
    totals, (results, grad_rows_all) = lax.scan(one_sequence, start_totals, (seq_inputs, seq_positions, seq_grads))
    full_shape = inputs.shape
    return (results.reshape(full_shape), grad_rows_all.reshape(full_shape), totals[0], totals[1], totals[2], totals[3], totals[4], totals[5], totals[6], totals[7], totals[8])
```

```python
import jax
import jax.numpy as jnp
from jax import lax
from jax.sharding import PartitionSpec as P

HEADS = 32
KV_HEADS = 4
HEAD_DIM = 64


NORM_EPS = 1e-05
ROPE_BASE = 10000.0
MASKED_SCORE = -1e30
LOW = jnp.bfloat16
WIDE = jnp.float32


def multiply(left, right):
    return jnp.dot(left, right, preferred_element_type=WIDE)


def against(left, right):
    return lax.dot_general(left, right, (((1,), (1,)), ((), ())), preferred_element_type=WIDE)


def outer_sum(left, right):
    return lax.dot_general(left, right, (((0,), (0,)), ((), ())), preferred_element_type=WIDE)


def swapped(block, distance, axis="ctx"):
    route = [(i, i ^ distance) for i in range(lax.axis_size(axis))]
    return lax.ppermute(block, axis, route)


def ctx_gather(block):
    size = lax.axis_size("ctx")
    if size != 4:
        return [block] + [swapped(block, k) for k in range(1, size)]
    half = block.shape[0] // 2
    from_x = swapped(block, 1)
    from_y = swapped(block, 2)
    far_top = swapped(from_x[:half], 2)
    far_low = swapped(from_y[half:], 1)
    return [block, from_x, from_y, jnp.concatenate([far_top, far_low], 0)]


def ctx_scatter_sum(parts):
    size = lax.axis_size("ctx")
    if size != 4:
        total = parts[0].astype(WIDE)
        for k in range(1, size):
            total = total + swapped(parts[k].astype(LOW), k).astype(WIDE)
        return total
    half = parts[0].shape[-1] // 2
    left = [part[:, :half] for part in parts]
    right = [part[:, half:] for part in parts]
    got_left = swapped(jnp.stack([left[1], left[3]]).astype(LOW), 1).astype(WIDE)
    got_right = swapped(jnp.stack([right[2], right[3]]).astype(LOW), 2).astype(WIDE)
    far_left = swapped((left[2].astype(WIDE) + got_left[1]).astype(LOW), 2).astype(WIDE)
    far_right = swapped((right[1].astype(WIDE) + got_right[1]).astype(LOW), 1).astype(WIDE)
    return jnp.concatenate(
        [
            left[0].astype(WIDE) + got_left[0] + far_left,
            right[0].astype(WIDE) + got_right[0] + far_right,
        ],
        -1,
    )


def in_rank_order(parts):
    me = lax.axis_index("ctx")
    stacked = jnp.stack(parts)
    return [
        lax.dynamic_index_in_dim(stacked, me ^ r, 0, keepdims=False) for r in range(len(parts))
    ]


def rows_to_columns(pick):
    me = lax.axis_index("ctx")
    size = lax.axis_size("ctx")
    parts = [pick(me)] + [swapped(pick(me ^ k), k) for k in range(1, size)]
    return jnp.concatenate(in_rank_order(parts), 0)


def columns_to_rows(block):
    me = lax.axis_index("ctx")
    size = lax.axis_size("ctx")
    rows = block.shape[0] // size
    pieces = [lax.dynamic_slice_in_dim(block, (me ^ k) * rows, rows, 0) for k in range(size)]
    return in_rank_order([pieces[0]] + [swapped(pieces[k], k) for k in range(1, size)])


def regrouped(block, back=False):
    dp_size, ctx_size = lax.axis_size("dp"), lax.axis_size("ctx")
    route = [(b, (b % dp_size) * ctx_size + b // dp_size) for b in range(dp_size * ctx_size)]
    if back:
        route = [(there, here) for here, there in route]
    return lax.ppermute(block, ("dp", "ctx"), route)


def dp_gather(block):
    return lax.all_gather(block, "dp", axis=0, tiled=True)


def dp_scatter_sum(block):
    return lax.psum_scatter(block, "dp", scatter_dimension=0, tiled=True)


def rotate(values, angles):
    cosine = jnp.cos(angles)
    sine = jnp.sin(angles)
    cosine = jnp.concatenate([cosine, cosine], -1)[:, None, :]
    sine = jnp.concatenate([sine, sine], -1)[:, None, :]
    half_dim = values.shape[-1] // 2
    turned = jnp.concatenate([-values[..., half_dim:], values[..., :half_dim]], -1)
    return values * cosine + turned * sine


def norm_scale(values):
    return lax.rsqrt(jnp.mean(values * values, -1, keepdims=True) + NORM_EPS)


def norm_back(grad_hidden, normed, scale_rows, gain):
    gain_grad = jnp.sum(grad_hidden * normed, 0)
    scaled = grad_hidden * gain
    return (
        gain_grad,
        scale_rows * (scaled - normed * jnp.mean(scaled * normed, -1, keepdims=True)),
    )


def split_rows(values, count):
    rows = values.shape[0] // count
    return [values[k * rows : (k + 1) * rows] for k in range(count)]


def local(
    inputs,
    positions,
    block_order,
    norm_attn,
    w_query,
    w_key,
    w_value,
    w_out,
    norm_mlp,
    w_gate,
    w_up,
    w_down,
    cotangent,
):
    row_count = inputs.shape[2]
    model_width = inputs.shape[3]
    block_rows = row_count // 2
    ctx_size = lax.axis_size("ctx")
    ctx_rank = lax.axis_index("ctx")
    head_dim = HEAD_DIM
    heads = HEADS // ctx_size
    sharers = ctx_size // KV_HEADS
    query_width = heads * head_dim
    ff_width = w_gate.shape[1] // ctx_size
    score_scale = head_dim ** (-0.5)
    both = ("dp", "ctx")

    x_low = inputs.reshape(row_count, model_width)
    grad_top = cotangent.reshape(row_count, model_width)
    x_parts = ctx_gather(x_low)
    gains = lax.all_gather(jnp.stack([norm_attn, norm_mlp]), both, axis=1, tiled=True).astype(WIDE)
    gain_attn, gain_mlp = gains[0], gains[1]

    def pick_attn(rank):
        kv_start = rank // sharers * head_dim
        return jnp.concatenate(
            [
                lax.dynamic_slice_in_dim(w_query, rank * query_width, query_width, 1),
                lax.dynamic_slice_in_dim(w_key, kv_start, head_dim, 1),
                lax.dynamic_slice_in_dim(w_value, kv_start, head_dim, 1),
            ],
            1,
        )

    def pick_mlp(rank):
        return jnp.concatenate(
            [
                lax.dynamic_slice_in_dim(w_gate, rank * ff_width, ff_width, 1),
                lax.dynamic_slice_in_dim(w_up, rank * ff_width, ff_width, 1),
            ],
            1,
        )

    part_qkv = dp_gather(rows_to_columns(pick_attn))
    part_out = dp_gather(regrouped(w_out))
    part_gate_up = dp_gather(rows_to_columns(pick_mlp))
    part_down = dp_gather(regrouped(w_down))
    part_gate, part_up = part_gate_up[:, :ff_width], part_gate_up[:, ff_width:]

    frequency = ROPE_BASE ** (-jnp.arange(head_dim // 2, dtype=WIDE) * 2.0 / head_dim)
    position_rows = positions.reshape(row_count)
    all_positions = jnp.concatenate(
        [position_rows] + [swapped(position_rows, k) for k in range(1, ctx_size)]
    )
    angles = all_positions.astype(WIDE)[:, None] * frequency[None, :]
    offsets = jnp.arange(block_rows, dtype=jnp.int32)
    index = jnp.concatenate(
        [
            (
                lax.dynamic_index_in_dim(block_order, ctx_rank ^ k, 0, keepdims=False)[:, None]
                * block_rows
                + offsets[None, :]
            ).reshape(row_count)
            for k in range(ctx_size)
        ]
    )
    visible = index[None, :] <= index[:, None]
    seq_rows = row_count * ctx_size

    x_all = jnp.concatenate(x_parts, 0).astype(WIDE)
    hidden_attn = (x_all * norm_scale(x_all) * gain_attn).astype(LOW)
    qkv = multiply(hidden_attn, part_qkv)
    queries = rotate(qkv[:, :query_width].reshape(seq_rows, heads, head_dim), angles).astype(LOW)
    keys = rotate(qkv[:, None, query_width : query_width + head_dim], angles)[:, 0].astype(LOW)
    values = qkv[:, query_width + head_dim :].astype(LOW)
    scores = jnp.einsum("qhd,kd->hqk", queries, keys, preferred_element_type=WIDE) * score_scale
    scores = jnp.where(visible, scores, MASKED_SCORE)
    maxima = jnp.max(scores, -1, keepdims=True)
    weights = jnp.exp(scores - maxima)
    totals = jnp.sum(weights, -1, keepdims=True)
    log_total = maxima + jnp.log(totals)
    probabilities = (weights / totals).astype(LOW)
    attended = jnp.einsum("hqk,kd->qhd", probabilities, values, preferred_element_type=WIDE)
    attn_low = attended.reshape(seq_rows, query_width).astype(LOW)

    x_rows = x_low.astype(WIDE)
    middle = x_rows + ctx_scatter_sum(split_rows(multiply(attn_low, part_out), ctx_size))
    scale_mlp = norm_scale(middle)
    normed_mlp = middle * scale_mlp
    hidden_mlp = jnp.concatenate(ctx_gather((normed_mlp * gain_mlp).astype(LOW)), 0)
    gate_rows = multiply(hidden_mlp, part_gate)
    up_rows = multiply(hidden_mlp, part_up)
    sigmoid_gate = jax.nn.sigmoid(gate_rows)
    swished = gate_rows * sigmoid_gate
    activated = (swished * up_rows).astype(LOW)

    top_all = jnp.concatenate(ctx_gather(grad_top), 0)
    grad_down = dp_scatter_sum(outer_sum(activated, top_all).astype(LOW))
    grad_activated = against(top_all, part_down)
    grad_gate = (
        grad_activated * up_rows * sigmoid_gate * (1.0 + gate_rows * (1.0 - sigmoid_gate))
    ).astype(LOW)
    grad_up = (grad_activated * swished).astype(LOW)
    grad_gate_up = jnp.concatenate([grad_gate, grad_up], 1)
    grad_hidden_mlp = ctx_scatter_sum(split_rows(against(grad_gate_up, part_gate_up), ctx_size))
    grad_gate_up_w = dp_scatter_sum(outer_sum(hidden_mlp, grad_gate_up).astype(LOW))
    gain_mlp_grad, grad_mid_norm = norm_back(grad_hidden_mlp, normed_mlp, scale_mlp, gain_mlp)
    grad_middle = grad_top.astype(WIDE) + grad_mid_norm
    result = middle + ctx_scatter_sum(split_rows(multiply(activated, part_down), ctx_size))
    outputs = result.astype(LOW).reshape(inputs.shape)

    grad_branch = jnp.concatenate(ctx_gather(grad_middle.astype(LOW)), 0)
    grad_out_w = dp_scatter_sum(outer_sum(attn_low, grad_branch).astype(LOW))
    grad_attn = against(grad_branch, part_out).astype(LOW)
    grad_heads = grad_attn.reshape(seq_rows, heads, head_dim)
    delta_rows = jnp.sum(grad_heads.astype(WIDE) * attended, -1).T[..., None]
    scores = jnp.einsum("qhd,kd->hqk", queries, keys, preferred_element_type=WIDE) * score_scale
    weights = jnp.where(visible, jnp.exp(scores - log_total), 0.0)
    grad_values = jnp.einsum(
        "hqk,qhd->kd", weights.astype(LOW), grad_heads, preferred_element_type=WIDE
    )
    grad_probs = jnp.einsum("qhd,kd->hqk", grad_heads, values, preferred_element_type=WIDE)
    grad_scores = (weights * (grad_probs - delta_rows)).astype(LOW)
    grad_queries = jnp.einsum("hqk,kd->qhd", grad_scores, keys, preferred_element_type=WIDE)
    grad_keys = jnp.einsum("hqk,qhd->kd", grad_scores, queries, preferred_element_type=WIDE)
    grad_queries = rotate(grad_queries * score_scale, -angles).reshape(seq_rows, query_width)
    grad_keys = rotate(grad_keys[:, None, :] * score_scale, -angles)[:, 0]
    grad_qkv = jnp.concatenate([grad_queries, grad_keys, grad_values], 1).astype(LOW)
    grad_hidden_attn = ctx_scatter_sum(split_rows(against(grad_qkv, part_qkv), ctx_size))
    grad_qkv_w = dp_scatter_sum(outer_sum(hidden_attn, grad_qkv).astype(LOW))
    scale_attn = norm_scale(x_rows)
    gain_attn_grad, grad_in_norm = norm_back(
        grad_hidden_attn, x_rows * scale_attn, scale_attn, gain_attn
    )
    grad_inputs = (grad_middle + grad_in_norm).reshape(inputs.shape)

    out_gains = lax.psum_scatter(
        jnp.stack([gain_attn_grad, gain_mlp_grad]), both, scatter_dimension=1, tiled=True
    )
    qkv_rows = columns_to_rows(grad_qkv_w)
    out_query = jnp.concatenate([part[:, :query_width] for part in qkv_rows], 1).astype(WIDE)
    kv_parts = [part[:, query_width:].astype(WIDE) for part in qkv_rows]
    kv_parts = [sum(kv_parts[g * sharers : (g + 1) * sharers]) for g in range(KV_HEADS)]
    out_key = jnp.concatenate([part[:, :head_dim] for part in kv_parts], 1)
    out_value = jnp.concatenate([part[:, head_dim:] for part in kv_parts], 1)
    mlp_rows = columns_to_rows(grad_gate_up_w)
    out_gate = jnp.concatenate([part[:, :ff_width] for part in mlp_rows], 1).astype(WIDE)
    out_up = jnp.concatenate([part[:, ff_width:] for part in mlp_rows], 1).astype(WIDE)
    out_out = regrouped(grad_out_w, back=True).astype(WIDE)
    out_down = regrouped(grad_down, back=True).astype(WIDE)
    return (
        outputs,
        grad_inputs,
        out_gains[0],
        out_query,
        out_key,
        out_value,
        out_out,
        out_gains[1],
        out_gate,
        out_up,
        out_down,
    )


def solution(mesh):
    placed = (
        P("dp", "ctx", None, None),
        P("dp", "ctx", None),
        P(),
        P(("dp", "ctx")),
        P(("dp", "ctx"), None),
        P(("dp", "ctx"), None),
        P(("dp", "ctx"), None),
        P(("dp", "ctx"), None),
        P(("dp", "ctx")),
        P(("dp", "ctx"), None),
        P(("dp", "ctx"), None),
        P(("dp", "ctx"), None),
        P("dp", "ctx", None, None),
    )
    return jax.shard_map(
        local,
        mesh=mesh,
        in_specs=placed,
        out_specs=(
            P("dp", "ctx", None, None),
            P("dp", "ctx", None, None),
            P(("dp", "ctx")),
            P(("dp", "ctx"), None),
            P(("dp", "ctx"), None),
            P(("dp", "ctx"), None),
            P(("dp", "ctx"), None),
            P(("dp", "ctx")),
            P(("dp", "ctx"), None),
            P(("dp", "ctx"), None),
            P(("dp", "ctx"), None),
        ),
        check_vma=False,
    )
```

```python
import functools

import jax
import jax.numpy as jnp
from jax import lax
from jax.experimental import pallas as pl
from jax.experimental.pallas import tpu as pltpu
from jax.sharding import PartitionSpec as P

HEADS = 32
KV_HEADS = 4
HEAD_DIM = 64
LANES = 2 * HEAD_DIM


NORM_EPS = 1e-05
ROPE_BASE = 10000.0
MASKED_SCORE = -1e30
LOW = jnp.bfloat16
WIDE = jnp.float32


def multiply(left, right):
    return jnp.dot(left, right, preferred_element_type=WIDE)


def against(left, right):
    return lax.dot_general(left, right, (((1,), (1,)), ((), ())), preferred_element_type=WIDE)


def outer_sum(left, right):
    return lax.dot_general(left, right, (((0,), (0,)), ((), ())), preferred_element_type=WIDE)


def swapped(block, distance, axis="ctx"):
    route = [(i, i ^ distance) for i in range(lax.axis_size(axis))]
    return lax.ppermute(block, axis, route)


def tied(*values):
    return lax.optimization_barrier(values)


def tied_lists(received, others):
    values = tied(*received, *others)
    return list(values[: len(received)]), list(values[len(received) :])


def ctx_gather(block, first=(), second=()):
    size = lax.axis_size("ctx")
    if size != 4:
        got = [swapped(block, k) for k in range(1, size)]
        got, others = tied_lists(got, [*first, *second])
        return [block] + got, others
    half = block.shape[0] // 2
    got = [swapped(block, 1), swapped(block, 2)]
    (from_x, from_y), first = tied_lists(got, first)
    got = [swapped(from_x[:half], 2), swapped(from_y[half:], 1)]
    far, second = tied_lists(got, second)
    return [block, from_x, from_y, jnp.concatenate(far, 0)], first + second


def ctx_scatter_sum(values, first=(), second=()):
    size = lax.axis_size("ctx")
    parts = split_rows(values, size)
    if size != 4:
        got = [swapped(parts[k].astype(LOW), k) for k in range(1, size)]
        got, others = tied_lists(got, [*first, *second])
        return sum([part.astype(WIDE) for part in got], parts[0].astype(WIDE)), others
    half = parts[0].shape[-1] // 2
    left = [part[:, :half] for part in parts]
    right = [part[:, half:] for part in parts]
    got = [
        swapped(jnp.stack([left[1], left[3]]).astype(LOW), 1),
        swapped(jnp.stack([right[2], right[3]]).astype(LOW), 2),
    ]
    (got_left, got_right), first = tied_lists(got, first)
    got_left, got_right = got_left.astype(WIDE), got_right.astype(WIDE)
    got = [
        swapped((left[2].astype(WIDE) + got_left[1]).astype(LOW), 2),
        swapped((right[1].astype(WIDE) + got_right[1]).astype(LOW), 1),
    ]
    (far_left, far_right), second = tied_lists(got, second)
    total = jnp.concatenate(
        [
            left[0].astype(WIDE) + got_left[0] + far_left.astype(WIDE),
            right[0].astype(WIDE) + got_right[0] + far_right.astype(WIDE),
        ],
        -1,
    )
    return total, first + second


def in_rank_order(parts):
    me = lax.axis_index("ctx")
    stacked = jnp.stack(parts)
    return [
        lax.dynamic_index_in_dim(stacked, me ^ r, 0, keepdims=False) for r in range(len(parts))
    ]


def exchanged(pick):
    me = lax.axis_index("ctx")
    return [pick(me)] + [swapped(pick(me ^ k), k) for k in range(1, lax.axis_size("ctx"))]


def columns_to_rows(block):
    me = lax.axis_index("ctx")
    size = lax.axis_size("ctx")
    rows = block.shape[0] // size
    pieces = [lax.dynamic_slice_in_dim(block, (me ^ k) * rows, rows, 0) for k in range(size)]
    return in_rank_order([pieces[0]] + [swapped(pieces[k], k) for k in range(1, size)])


def regrouped(block, back=False):
    dp_size, ctx_size = lax.axis_size("dp"), lax.axis_size("ctx")
    route = [(b, (b % dp_size) * ctx_size + b // dp_size) for b in range(dp_size * ctx_size)]
    if back:
        route = [(there, here) for here, there in route]
    return lax.ppermute(block, ("dp", "ctx"), route)


def dp_gather(block):
    return lax.all_gather(block, "dp", axis=0, tiled=True)


def dp_scatter_sum(block):
    return lax.psum_scatter(block, "dp", scatter_dimension=0, tiled=True)


def lane_of(shape):
    return lax.broadcasted_iota(jnp.int32, shape, 1)


def turned(values):
    first = lane_of(values.shape) % HEAD_DIM < HEAD_DIM // 2
    return jnp.where(
        first,
        pltpu.roll(values, LANES - HEAD_DIM // 2, 1),
        pltpu.roll(values, HEAD_DIM // 2, 1),
    )


def both_heads(pair):
    even = lane_of(pair.shape) < HEAD_DIM
    zero = jnp.zeros_like(pair)
    return jnp.concatenate([jnp.where(even, pair, zero), jnp.where(even, zero, pair)], 0)


def one_pair(stacked):
    rows = stacked.shape[0] // 2
    even = lane_of((rows, LANES)) < HEAD_DIM
    return jnp.where(even, stacked[:rows], stacked[rows:])


def seen(rows, chunk, last_key):
    query = lax.broadcasted_iota(jnp.int32, (rows, chunk), 0) % (chunk // 2)
    key = lax.broadcasted_iota(jnp.int32, (rows, chunk), 1)
    return key <= query + last_key


def attend_kernel(pairs, chunk, order, q_ref, kv_ref, cos_ref, sin_ref, cosb_ref, sinb_ref,
                  out_ref, rot_ref, keys_ref, values_ref, lse_ref):
    rows = chunk // 2
    step = pl.program_id(0)
    chunks = keys_ref.shape[0] // chunk

    @pl.when(step == 0)
    def _():
        for b in range(keys_ref.shape[0] // rows):
            here = slice(b * rows, (b + 1) * rows)
            there = pl.ds(pl.multiple_of(order[b] * rows, rows), rows)
            own = kv_ref[here, :]
            other = pltpu.roll(own, HEAD_DIM, 1)
            low = lane_of(own.shape) < HEAD_DIM
            keys = jnp.where(low, own, other)
            keys = keys * cos_ref[here, :] + turned(keys) * sin_ref[here, :]
            keys_ref[there, :] = keys.astype(LOW)
            values_ref[there, :] = jnp.where(low, other, own).astype(LOW)

    cosine, sine = cosb_ref[...], sinb_ref[...]
    place = order[step]
    last_key = (place % 2) * rows
    for p in range(pairs):
        lanes = slice(p * LANES, (p + 1) * LANES)
        pair = q_ref[:, lanes]
        pair = pair * cosine + turned(pair) * sine
        rot_ref[:, lanes] = (pair.astype(LOW).astype(WIDE) * HEAD_DIM**-0.5).astype(LOW)

    for count in range(1, chunks + 1):

        @pl.when(place // 2 == count - 1)
        def _(count=count):
            visible = seen(2 * rows, chunk, last_key)
            all_lse = jnp.zeros((rows, LANES), WIDE)
            lane = lane_of((rows, LANES))
            for p in range(pairs):
                lanes = slice(p * LANES, (p + 1) * LANES)
                queries = both_heads(rot_ref[:, lanes])
                scores = [
                    against(queries, keys_ref[c * chunk : (c + 1) * chunk, :]) for c in range(count)
                ]
                scores[-1] = jnp.where(visible, scores[-1], MASKED_SCORE)
                top = jnp.max(functools.reduce(jnp.maximum, scores), 1, keepdims=True)
                weights = [jnp.exp(s - top) for s in scores]
                total = jnp.sum(functools.reduce(jnp.add, weights), 1, keepdims=True)
                mixture = sum(
                    multiply(w.astype(LOW), values_ref[c * chunk : (c + 1) * chunk, :])
                    for c, w in enumerate(weights)
                )
                out_ref[:, lanes] = one_pair(mixture / total).astype(LOW)
                lse = top + jnp.log(total)
                all_lse = jnp.where(lane == 2 * p, lse[:rows], all_lse)
                all_lse = jnp.where(lane == 2 * p + 1, lse[rows:], all_lse)
            lse_ref[...] = all_lse


def attend_back_kernel(pairs, chunk, order, rot_ref, grad_ref, out_ref, lse_ref, cosb_ref, sinb_ref,
                       keys_ref, values_ref, cos_ref, sin_ref, dqkv_ref, dkeys, dvalues, flat):
    rows = chunk // 2
    step = pl.program_id(0)
    steps = pl.num_programs(0)
    chunks = keys_ref.shape[0] // chunk
    scale = HEAD_DIM**-0.5

    @pl.when(step == 0)
    def _():
        dkeys[...] = jnp.zeros_like(dkeys)
        dvalues[...] = jnp.zeros_like(dvalues)

    place = order[step]
    last_chunk = place // 2
    last_key = (place % 2) * rows
    here = pl.ds(pl.multiple_of(step * rows, rows), rows)
    queries, grads, lses, deltas = [], [], [], []
    for p in range(pairs):
        lanes = slice(p * LANES, (p + 1) * LANES)
        queries.append(both_heads(rot_ref[:, lanes]))
        grads.append(both_heads(grad_ref[:, lanes]))
        product = grad_ref[:, lanes].astype(WIDE) * out_ref[:, lanes].astype(WIDE)
        low = lane_of(product.shape) < HEAD_DIM
        deltas.append(
            jnp.concatenate(
                [
                    jnp.sum(jnp.where(low, product, 0.0), 1, keepdims=True),
                    jnp.sum(jnp.where(low, 0.0, product), 1, keepdims=True),
                ],
                0,
            )
        )
        lses.append(
            jnp.concatenate(
                [lse_ref[:, 2 * p : 2 * p + 1], lse_ref[:, 2 * p + 1 : 2 * p + 2]], 0
            )
        )
    queries_t = [q.T for q in queries]
    grads_t = [g.T for g in grads]

    def one_chunk(c, dq, masked):
        place_c = pl.ds(pl.multiple_of(c * chunk, chunk), chunk)
        keys = keys_ref[place_c, :]
        values = values_ref[place_c, :]
        dk = dkeys[c]
        dv = dvalues[c]
        new = []
        for p in range(pairs):
            weights = jnp.exp(against(queries[p], keys) - lses[p])
            if masked:
                weights = jnp.where(seen(2 * rows, chunk, last_key), weights, 0.0)
            slopes = against(grads[p], values)
            ds = (weights * (slopes - deltas[p])).astype(LOW)
            new.append(dq[p] + multiply(ds, keys))
            dk = dk + multiply(queries_t[p], ds)
            dv = dv + multiply(grads_t[p], weights.astype(LOW))
        dkeys[c] = dk
        dvalues[c] = dv
        return tuple(new)

    start = tuple(jnp.zeros((2 * rows, LANES), WIDE) for _ in range(pairs))
    dq = lax.fori_loop(0, last_chunk, lambda c, d: one_chunk(c, d, False), start)
    dq = one_chunk(last_chunk, dq, True)
    cosine, sine = cosb_ref[...], sinb_ref[...]
    for p in range(pairs):
        pair = one_pair(dq[p]) * scale
        pair = pair * cosine - turned(pair) * sine
        dqkv_ref[here, p * LANES : (p + 1) * LANES] = pair.astype(LOW)

    @pl.when(step == steps - 1)
    def _():
        for c in range(chunks):
            dk, dv = dkeys[c], dvalues[c]
            side = jnp.concatenate(
                [dk[:HEAD_DIM] + dk[HEAD_DIM:], dv[:HEAD_DIM] + dv[HEAD_DIM:]], 0
            )
            flat[c * chunk : (c + 1) * chunk, :] = side.T
        for b in range(keys_ref.shape[0] // rows):
            mine = slice(b * rows, (b + 1) * rows)
            there = pl.ds(pl.multiple_of(order[b] * rows, rows), rows)
            own = flat[there, :]
            back = own * cos_ref[mine, :] - turned(own) * sin_ref[mine, :]
            low = lane_of(own.shape) < HEAD_DIM
            dqkv_ref[mine, pairs * LANES :] = jnp.where(low, back, own).astype(LOW)


def attend(order, qkv, cosine, sine, rows):
    seq, width = qkv.shape[0], qkv.shape[1] - LANES
    pairs = width // LANES
    blocks = seq // rows
    block = lambda w: pl.BlockSpec((rows, w), lambda i, _: (i, 0))
    whole = lambda w, at=0: pl.BlockSpec((seq, w), lambda i, _: (0, at))
    return pl.pallas_call(
        functools.partial(attend_kernel, pairs, 2 * rows),
        grid_spec=pltpu.PrefetchScalarGridSpec(
            num_scalar_prefetch=1,
            grid=(blocks,),
            in_specs=[block(width), whole(LANES, pairs), whole(LANES), whole(LANES), block(LANES), block(LANES)],
            out_specs=[block(width), block(width), whole(LANES), whole(LANES), block(LANES)],
        ),
        out_shape=[
            jax.ShapeDtypeStruct((seq, width), LOW),
            jax.ShapeDtypeStruct((seq, width), LOW),
            jax.ShapeDtypeStruct((seq, LANES), LOW),
            jax.ShapeDtypeStruct((seq, LANES), LOW),
            jax.ShapeDtypeStruct((seq, LANES), WIDE),
        ],
        compiler_params=pltpu.CompilerParams(vmem_limit_bytes=48 << 20),
        cost_estimate=pl.CostEstimate(flops=2 * 2 * seq * seq * width, bytes_accessed=8 << 20, transcendentals=seq * seq * width // HEAD_DIM // 2),
        name="attend",
    )(order, qkv, qkv, cosine, sine, cosine, sine)


def attend_back(order, rotated, grad, out, lse, keys, values, cosine, sine, rows):
    seq, width = rotated.shape
    pairs = width // LANES
    blocks = seq // rows
    block = lambda w: pl.BlockSpec((rows, w), lambda i, _: (i, 0))
    whole = lambda w: pl.BlockSpec((seq, w), lambda i, _: (0, 0))
    chunks = seq // (2 * rows)
    return pl.pallas_call(
        functools.partial(attend_back_kernel, pairs, 2 * rows),
        grid_spec=pltpu.PrefetchScalarGridSpec(
            num_scalar_prefetch=1,
            grid=(blocks,),
            in_specs=[block(width), block(width), block(width), block(LANES), block(LANES), block(LANES),
                      whole(LANES), whole(LANES), whole(LANES), whole(LANES)],
            out_specs=whole(width + LANES),
            scratch_shapes=[
                pltpu.VMEM((chunks, LANES, 2 * rows), WIDE),
                pltpu.VMEM((chunks, LANES, 2 * rows), WIDE),
                pltpu.VMEM((seq, LANES), WIDE),
            ],
        ),
        out_shape=jax.ShapeDtypeStruct((seq, width + LANES), LOW),
        compiler_params=pltpu.CompilerParams(vmem_limit_bytes=48 << 20),
        cost_estimate=pl.CostEstimate(flops=5 * 2 * seq * seq * width, bytes_accessed=8 << 20, transcendentals=seq * seq * width // HEAD_DIM // 2),
        name="attend_back",
    )(order, rotated, grad, out, lse, cosine, sine, keys, values, cosine, sine)


def fold_kernel(count, cuts, qkv_ref, out_ref, joined_ref):
    rows, cut = out_ref.shape[0] // count, out_ref.shape[1] // cuts
    width = qkv_ref.shape[1]
    joined_ref[:, :width] = qkv_ref[...]
    for d in range(count):
        for j in range(cuts):
            there = (d * cuts + j) * rows
            joined_ref[there : there + rows, width:] = out_ref[
                d * rows : (d + 1) * rows, j * cut : (j + 1) * cut
            ]


def fold(qkv, out, count):
    cuts = qkv.shape[0] // out.shape[0]
    width = qkv.shape[1] + out.shape[1] // cuts
    return pl.pallas_call(
        functools.partial(fold_kernel, count, cuts),
        out_shape=jax.ShapeDtypeStruct((qkv.shape[0], width), qkv.dtype),
        compiler_params=pltpu.CompilerParams(vmem_limit_bytes=40 << 20),
        name="fold",
    )(qkv, out)


def unfold_kernel(count, cuts, joined_ref, qkv_ref, out_ref):
    rows, cut = out_ref.shape[0] // count, out_ref.shape[1] // cuts
    width = qkv_ref.shape[1]
    qkv_ref[...] = joined_ref[:, :width]
    for d in range(count):
        for j in range(cuts):
            there = (d * cuts + j) * rows
            out_ref[d * rows : (d + 1) * rows, j * cut : (j + 1) * cut] = joined_ref[
                there : there + rows, width:
            ]


def unfold(joined, cut, cuts, count):
    rows, width = joined.shape
    return pl.pallas_call(
        functools.partial(unfold_kernel, count, cuts),
        out_shape=[
            jax.ShapeDtypeStruct((rows, width - cut), joined.dtype),
            jax.ShapeDtypeStruct((rows // cuts, cut * cuts), joined.dtype),
        ],
        compiler_params=pltpu.CompilerParams(vmem_limit_bytes=40 << 20),
        name="unfold",
    )(joined)


def spread_kernel(dp_size, chunk, gate_ref, up_ref, out_ref):
    ranks, _, width = out_ref.shape
    for side, ref in enumerate((gate_ref, up_ref)):
        for r in range(ranks):
            for d in range(dp_size):
                here = side * width // 2 + d * chunk
                there = (d * ranks + r) * chunk
                out_ref[r, :, here : here + chunk] = ref[:, there : there + chunk]


def merge_kernel(dp_size, chunk, parts_ref, gate_ref, up_ref):
    ranks, _, width = parts_ref.shape
    for side, ref in enumerate((gate_ref, up_ref)):
        for r in range(ranks):
            for d in range(dp_size):
                here = side * width // 2 + d * chunk
                there = (d * ranks + r) * chunk
                ref[:, there : there + chunk] = parts_ref[r, :, here : here + chunk].astype(WIDE)


def spread(gate, up, dp_size, ctx_size, chunk):
    shape = (ctx_size, gate.shape[0], 2 * dp_size * chunk)
    return pl.pallas_call(
        functools.partial(spread_kernel, dp_size, chunk),
        out_shape=jax.ShapeDtypeStruct(shape, gate.dtype),
        name="spread",
    )(gate, up)


def merge(parts, dp_size, chunk):
    shape = jax.ShapeDtypeStruct((parts.shape[1], parts.shape[0] * dp_size * chunk), WIDE)
    return pl.pallas_call(
        functools.partial(merge_kernel, dp_size, chunk), out_shape=[shape, shape], name="merge"
    )(parts)


def norm_scale(values):
    return lax.rsqrt(jnp.mean(values * values, -1, keepdims=True) + NORM_EPS)


def norm_back(grad_hidden, normed, scale_rows, gain):
    gain_grad = jnp.sum(grad_hidden * normed, 0)
    scaled = grad_hidden * gain
    return (
        gain_grad,
        scale_rows * (scaled - normed * jnp.mean(scaled * normed, -1, keepdims=True)),
    )


def split_rows(values, count):
    rows = values.shape[0] // count
    return [values[k * rows : (k + 1) * rows] for k in range(count)]


def local(
    inputs,
    positions,
    block_order,
    norm_attn,
    w_query,
    w_key,
    w_value,
    w_out,
    norm_mlp,
    w_gate,
    w_up,
    w_down,
    cotangent,
):
    row_count = inputs.shape[2]
    model_width = inputs.shape[3]
    block_rows = row_count // 2
    dp_size, ctx_size = lax.axis_size("dp"), lax.axis_size("ctx")
    ctx_rank = lax.axis_index("ctx")
    head_dim = HEAD_DIM
    sharers = ctx_size // KV_HEADS
    query_width = HEADS // ctx_size * head_dim
    qkv_width = query_width + 2 * head_dim
    ff_width = w_gate.shape[1] // ctx_size
    ff_chunk = w_down.shape[0]

    x_low = inputs.reshape(row_count, model_width)
    grad_top = cotangent.reshape(row_count, model_width)
    gain_rows = norm_attn.shape[0]
    own_positions = positions.reshape(gain_rows, -1)
    position_width = own_positions.shape[1]
    own_extras = jnp.concatenate(
        [
            jnp.stack([norm_attn, norm_mlp], 1),
            (own_positions // LANES).astype(LOW),
            (own_positions % LANES).astype(LOW),
        ],
        1,
    )
    own_extras = jnp.pad(own_extras, ((0, 0), (0, LANES - own_extras.shape[1])))

    def pick_attn(rank):
        kv_start = rank // sharers * head_dim
        return jnp.concatenate(
            [
                lax.dynamic_slice_in_dim(w_query, rank * query_width, query_width, 1),
                lax.dynamic_slice_in_dim(w_key, kv_start, head_dim, 1),
                lax.dynamic_slice_in_dim(w_value, kv_start, head_dim, 1),
                own_extras,
            ],
            1,
        )

    cuts = model_width // query_width
    parts_qkv = exchanged(pick_attn)
    parts_qkv, (block_out, x_low, columns) = tied_lists(
        parts_qkv,
        [regrouped(w_out), x_low, spread(w_gate, w_up, dp_size, ctx_size, ff_chunk)],
    )
    block_qkv = jnp.concatenate(in_rank_order(parts_qkv), 0)
    gathered_attn = dp_gather(fold(block_qkv, block_out, 1))
    x_parts, _ = ctx_gather(x_low)
    x_parts, (columns,) = tied_lists(x_parts, [columns])
    x_all = jnp.concatenate(x_parts, 0)
    parts_gate_up = exchanged(
        lambda rank: lax.dynamic_index_in_dim(columns, rank, 0, keepdims=False)
    )
    gathered_qkv, part_out = unfold(gathered_attn, query_width, cuts, dp_size)
    part_qkv = gathered_qkv[:, :qkv_width]
    gains = gathered_qkv[:, qkv_width:].astype(WIDE).T
    gain_attn, gain_mlp = gains[0], gains[1]

    sent = block_qkv.reshape(ctx_size, gain_rows, -1)[:, :, qkv_width + 2 :].astype(WIDE)
    sent = LANES * sent[..., :position_width] + sent[..., position_width : 2 * position_width]
    sent = sent.reshape(ctx_size, row_count)
    ranks = [ctx_rank ^ k for k in range(ctx_size)]
    all_positions = jnp.concatenate(
        [lax.dynamic_index_in_dim(sent, r, 0, keepdims=False) for r in ranks]
    )
    frequency = ROPE_BASE ** (-jnp.arange(head_dim // 2, dtype=WIDE) * 2.0 / head_dim)
    angles = all_positions[:, None] * frequency[None, :]
    cosine = jnp.tile(jnp.cos(angles), (1, 4))
    sine = jnp.sin(angles)
    sine = jnp.concatenate([-sine, sine, -sine, sine], 1)
    order = jnp.concatenate([block_order[r] for r in ranks])

    x_wide = x_all.astype(WIDE)
    normed_attn = x_wide * norm_scale(x_wide)
    hidden_attn = (normed_attn * gain_attn).astype(LOW)
    (qkv,), parts_gate_up = tied_lists([multiply(hidden_attn, part_qkv)], parts_gate_up)
    part_gate_up = dp_gather(jnp.concatenate(in_rank_order(parts_gate_up), 0))
    attn_low, rotated, keys, values, log_total = attend(order, qkv, cosine, sine, block_rows)
    part_mixed = multiply(attn_low, part_out).astype(LOW)

    x_rows = x_low.astype(WIDE)
    mixed, _ = ctx_scatter_sum(part_mixed)
    middle, w_down = tied(x_rows + mixed, w_down)
    part_down = dp_gather(w_down)
    scale_mlp = norm_scale(middle)
    normed_mlp = middle * scale_mlp
    hidden_parts, _ = ctx_gather((normed_mlp * gain_mlp).astype(LOW))
    hidden_parts, (grad_top,) = tied_lists(hidden_parts, [grad_top])
    hidden_mlp = jnp.concatenate(hidden_parts, 0)
    gate_rows = multiply(hidden_mlp, part_gate_up[:, :ff_width])
    up_rows = multiply(hidden_mlp, part_gate_up[:, ff_width:])
    sigmoid_gate = jax.nn.sigmoid(gate_rows)
    swished = gate_rows * sigmoid_gate
    top_parts, (gate_rows, activated) = ctx_gather(
        grad_top, [gate_rows], [(swished * up_rows).astype(LOW)]
    )
    top_all = jnp.concatenate(top_parts, 0)
    part_down_w, part_down = tied(outer_sum(activated, top_all).astype(LOW), part_down)
    grad_down = dp_scatter_sum(part_down_w)

    grad_activated = against(top_all, part_down)
    grad_gate = (
        grad_activated * up_rows * sigmoid_gate * (1.0 + gate_rows * (1.0 - sigmoid_gate))
    ).astype(LOW)
    grad_up = (grad_activated * swished).astype(LOW)
    grad_gate_up = jnp.concatenate([grad_gate, grad_up], 1)
    part_hidden_mlp, grad_gate_up = tied(
        against(grad_gate_up, part_gate_up).astype(LOW), grad_gate_up
    )
    grad_hidden_mlp, (part_gate_up_w,) = ctx_scatter_sum(
        part_hidden_mlp, [outer_sum(hidden_mlp, grad_gate_up).astype(LOW)]
    )
    grad_gate_up_w = dp_scatter_sum(part_gate_up_w)
    gain_mlp_grad, grad_mid_norm = norm_back(grad_hidden_mlp, normed_mlp, scale_mlp, gain_mlp)
    grad_middle = grad_top.astype(WIDE) + grad_mid_norm

    branch_parts, (part_result, grad_down) = ctx_gather(
        grad_middle.astype(LOW), [multiply(activated, part_down).astype(LOW)], [grad_down]
    )
    grad_branch = jnp.concatenate(branch_parts, 0)
    grad_attn, part_result = tied(against(grad_branch, part_out).astype(LOW), part_result)
    grad_qkv = attend_back(
        order, rotated, grad_attn, attn_low, log_total, keys, values, cosine, sine, block_rows
    )
    part_result, (grad_qkv,) = ctx_scatter_sum(part_result, [grad_qkv])
    outputs = (middle + part_result).astype(LOW).reshape(inputs.shape)
    part_hidden_attn = against(grad_qkv, part_qkv)
    gain_attn_grad = jnp.sum(part_hidden_attn * normed_attn, 0)
    gain_grads = jnp.pad(
        jnp.stack([gain_attn_grad, gain_mlp_grad], 1).astype(LOW), ((0, 0), (0, LANES - 2))
    )
    part_hidden_attn, grad_qkv, outputs = tied(part_hidden_attn.astype(LOW), grad_qkv, outputs)
    part_qkv_w = jnp.concatenate([outer_sum(hidden_attn, grad_qkv).astype(LOW), gain_grads], 1)
    part_out_w = outer_sum(attn_low, grad_branch).astype(LOW)
    grad_hidden_attn, (part_attn_w,) = ctx_scatter_sum(
        part_hidden_attn, [fold(part_qkv_w, part_out_w, dp_size)]
    )
    grad_attn_w = dp_scatter_sum(part_attn_w)
    scale_attn = norm_scale(x_rows)
    _, grad_in_norm = norm_back(grad_hidden_attn, x_rows * scale_attn, scale_attn, gain_attn)
    grad_inputs = (grad_middle + grad_in_norm).reshape(inputs.shape)

    gate_up_rows = jnp.stack(columns_to_rows(grad_gate_up_w))
    out_gate, out_up = merge(gate_up_rows, dp_size, ff_chunk)
    out_down = grad_down.astype(WIDE)
    grad_attn_w, out_gate, out_up, grad_inputs = tied(grad_attn_w, out_gate, out_up, grad_inputs)
    grad_qkv_w, grad_out_w = unfold(grad_attn_w, query_width, cuts, 1)
    out_out = regrouped(grad_out_w, back=True).astype(WIDE)
    qkv_rows = columns_to_rows(grad_qkv_w)
    out_query = jnp.concatenate([part[:, :query_width] for part in qkv_rows], 1).astype(WIDE)
    rests = [part[:, query_width:].astype(WIDE) for part in qkv_rows]
    kv_parts = [sum(rests[g * sharers : (g + 1) * sharers]) for g in range(KV_HEADS)]
    out_key = jnp.concatenate([part[:, :head_dim] for part in kv_parts], 1)
    out_value = jnp.concatenate([part[:, head_dim : 2 * head_dim] for part in kv_parts], 1)
    out_gains = sum(rests)[:, 2 * head_dim : 2 * head_dim + 2].T
    return (
        outputs,
        grad_inputs,
        out_gains[0],
        out_query,
        out_key,
        out_value,
        out_out,
        out_gains[1],
        out_gate,
        out_up,
        out_down,
    )


def solution(mesh):
    placed = (
        P("dp", "ctx", None, None),
        P("dp", "ctx", None),
        P(),
        P(("dp", "ctx")),
        P(("dp", "ctx"), None),
        P(("dp", "ctx"), None),
        P(("dp", "ctx"), None),
        P(("dp", "ctx"), None),
        P(("dp", "ctx")),
        P(("dp", "ctx"), None),
        P(("dp", "ctx"), None),
        P(("dp", "ctx"), None),
        P("dp", "ctx", None, None),
    )
    return jax.shard_map(
        local,
        mesh=mesh,
        in_specs=placed,
        out_specs=(
            P("dp", "ctx", None, None),
            P("dp", "ctx", None, None),
            P(("dp", "ctx")),
            P(("dp", "ctx"), None),
            P(("dp", "ctx"), None),
            P(("dp", "ctx"), None),
            P(("dp", "ctx"), None),
            P(("dp", "ctx")),
            P(("dp", "ctx"), None),
            P(("dp", "ctx"), None),
            P(("dp", "ctx"), None),
        ),
        check_vma=False,
    )
```

```python
import functools

import jax
import jax.numpy as jnp
from jax import lax
from jax.experimental import pallas as pl
from jax.experimental.pallas import tpu as pltpu
from jax.sharding import PartitionSpec as P

HEADS = 32
KV_HEADS = 4
HEAD_DIM = 64
LANES = 2 * HEAD_DIM


NORM_EPS = 1e-05
ROPE_BASE = 10000.0
MASKED_SCORE = -1e30
LOW = jnp.bfloat16
WIDE = jnp.float32


def multiply(left, right):
    return jnp.dot(left, right, preferred_element_type=WIDE)


def against(left, right):
    return lax.dot_general(left, right, (((1,), (1,)), ((), ())), preferred_element_type=WIDE)


def outer_sum(left, right):
    return lax.dot_general(left, right, (((0,), (0,)), ((), ())), preferred_element_type=WIDE)


def swapped(block, distance, axis="ctx"):
    route = [(i, i ^ distance) for i in range(lax.axis_size(axis))]
    return lax.ppermute(block, axis, route)


def tied(*values):
    return lax.optimization_barrier(values)


def tied_lists(received, others):
    values = tied(*received, *others)
    return list(values[: len(received)]), list(values[len(received) :])


def ctx_gather(block, first=(), second=()):
    size = lax.axis_size("ctx")
    if size != 4:
        got = [swapped(block, k) for k in range(1, size)]
        second = second(*first) if callable(second) else second
        got, others = tied_lists(got, [*first, *second])
        return [block] + got, others
    top, low = split_rows(block, 2)
    near = [swapped(top, 1), swapped(low, 2)]
    late = [swapped(low, 1), swapped(top, 2)]
    near, first = tied_lists(near, first)
    far = [swapped(near[0], 2), swapped(near[1], 1)]
    second = second(*first) if callable(second) else second
    got, second = tied_lists(late + far, second)
    return [block, near[0], *got[:2], near[1], *got[2:]], first + second


def ctx_scatter_sum(values, first=(), second=()):
    size = lax.axis_size("ctx")
    parts = split_rows(values, size)
    if size != 4:
        got = [swapped(parts[k].astype(LOW), k) for k in range(1, size)]
        got, others = tied_lists(got, [*first, *second])
        return sum([part.astype(WIDE) for part in got], parts[0].astype(WIDE)), others
    half = parts[0].shape[-1] // 2
    left = [part[:, :half] for part in parts]
    right = [part[:, half:] for part in parts]
    got = [
        swapped(jnp.stack([left[1], left[3]]).astype(LOW), 1),
        swapped(jnp.stack([right[2], right[3]]).astype(LOW), 2),
    ]
    (got_left, got_right), first = tied_lists(got, first)
    got_left, got_right = got_left.astype(WIDE), got_right.astype(WIDE)
    got = [
        swapped((left[2].astype(WIDE) + got_left[1]).astype(LOW), 2),
        swapped((right[1].astype(WIDE) + got_right[1]).astype(LOW), 1),
    ]
    (far_left, far_right), second = tied_lists(got, second)
    total = jnp.concatenate(
        [
            left[0].astype(WIDE) + got_left[0] + far_left.astype(WIDE),
            right[0].astype(WIDE) + got_right[0] + far_right.astype(WIDE),
        ],
        -1,
    )
    return total, first + second


def in_rank_order(parts):
    me = lax.axis_index("ctx")
    stacked = jnp.stack(parts)
    return [
        lax.dynamic_index_in_dim(stacked, me ^ r, 0, keepdims=False) for r in range(len(parts))
    ]


def exchanged(pick):
    me = lax.axis_index("ctx")
    return [pick(me)] + [swapped(pick(me ^ k), k) for k in range(1, lax.axis_size("ctx"))]


def columns_to_rows(block):
    me = lax.axis_index("ctx")
    size = lax.axis_size("ctx")
    rows = block.shape[0] // size
    pieces = [lax.dynamic_slice_in_dim(block, (me ^ k) * rows, rows, 0) for k in range(size)]
    return in_rank_order([pieces[0]] + [swapped(pieces[k], k) for k in range(1, size)])


def dp_gather(block):
    return lax.all_gather(block, "dp", axis=0, tiled=True)


def dp_scatter_sum(block):
    return lax.psum_scatter(block, "dp", scatter_dimension=0, tiled=True)


def lane_of(shape):
    return lax.broadcasted_iota(jnp.int32, shape, 1)


def turned(values):
    first = lane_of(values.shape) % HEAD_DIM < HEAD_DIM // 2
    return jnp.where(
        first,
        pltpu.roll(values, LANES - HEAD_DIM // 2, 1),
        pltpu.roll(values, HEAD_DIM // 2, 1),
    )


def both_heads(pair):
    even = lane_of(pair.shape) < HEAD_DIM
    zero = jnp.zeros_like(pair)
    return jnp.concatenate([jnp.where(even, pair, zero), jnp.where(even, zero, pair)], 0)


def one_pair(stacked):
    rows = stacked.shape[0] // 2
    even = lane_of((rows, LANES)) < HEAD_DIM
    return jnp.where(even, stacked[:rows], stacked[rows:])


def seen(rows, chunk, last_key):
    query = lax.broadcasted_iota(jnp.int32, (rows, chunk), 0) % (chunk // 2)
    key = lax.broadcasted_iota(jnp.int32, (rows, chunk), 1)
    return key <= query + last_key


def attend_kernel(pairs, chunk, order, q_ref, kv_ref, cos_ref, sin_ref, cosb_ref, sinb_ref,
                  out_ref, rot_ref, keys_ref, values_ref, lse_ref):
    rows = chunk // 2
    step = pl.program_id(0)
    chunks = keys_ref.shape[0] // chunk

    @pl.when(step == 0)
    def _():
        for b in range(keys_ref.shape[0] // rows):
            here = slice(b * rows, (b + 1) * rows)
            there = pl.ds(pl.multiple_of(order[b] * rows, rows), rows)
            own = kv_ref[here, :]
            other = pltpu.roll(own, HEAD_DIM, 1)
            low = lane_of(own.shape) < HEAD_DIM
            keys = jnp.where(low, own, other)
            keys = keys * cos_ref[here, :] + turned(keys) * sin_ref[here, :]
            keys_ref[there, :] = keys.astype(LOW)
            values_ref[there, :] = jnp.where(low, other, own).astype(LOW)

    cosine, sine = cosb_ref[...], sinb_ref[...]
    place = order[step]
    last_key = (place % 2) * rows
    for p in range(pairs):
        lanes = slice(p * LANES, (p + 1) * LANES)
        pair = q_ref[:, lanes]
        pair = pair * cosine + turned(pair) * sine
        rot_ref[:, lanes] = (pair.astype(LOW).astype(WIDE) * HEAD_DIM**-0.5).astype(LOW)

    for count in range(1, chunks + 1):

        @pl.when(place // 2 == count - 1)
        def _(count=count):
            visible = seen(2 * rows, chunk, last_key)
            all_lse = jnp.zeros((rows, LANES), WIDE)
            lane = lane_of((rows, LANES))
            for p in range(pairs):
                lanes = slice(p * LANES, (p + 1) * LANES)
                queries = both_heads(rot_ref[:, lanes])
                scores = [
                    against(queries, keys_ref[c * chunk : (c + 1) * chunk, :]) for c in range(count)
                ]
                scores[-1] = jnp.where(visible, scores[-1], MASKED_SCORE)
                top = jnp.max(functools.reduce(jnp.maximum, scores), 1, keepdims=True)
                weights = [jnp.exp(s - top) for s in scores]
                total = jnp.sum(functools.reduce(jnp.add, weights), 1, keepdims=True)
                mixture = sum(
                    multiply(w.astype(LOW), values_ref[c * chunk : (c + 1) * chunk, :])
                    for c, w in enumerate(weights)
                )
                out_ref[:, lanes] = one_pair(mixture / total).astype(LOW)
                lse = top + jnp.log(total)
                all_lse = jnp.where(lane == 2 * p, lse[:rows], all_lse)
                all_lse = jnp.where(lane == 2 * p + 1, lse[rows:], all_lse)
            lse_ref[...] = all_lse


def attend_back_kernel(pairs, chunk, order, rot_ref, grad_ref, out_ref, lse_ref, cosb_ref, sinb_ref,
                       keys_ref, values_ref, cos_ref, sin_ref, dqkv_ref, dkeys, dvalues, flat):
    rows = chunk // 2
    step = pl.program_id(0)
    steps = pl.num_programs(0)
    chunks = keys_ref.shape[0] // chunk
    scale = HEAD_DIM**-0.5

    @pl.when(step == 0)
    def _():
        dkeys[...] = jnp.zeros_like(dkeys)
        dvalues[...] = jnp.zeros_like(dvalues)

    place = order[step]
    last_chunk = place // 2
    last_key = (place % 2) * rows
    here = pl.ds(pl.multiple_of(step * rows, rows), rows)
    queries, grads, lses, deltas = [], [], [], []
    for p in range(pairs):
        lanes = slice(p * LANES, (p + 1) * LANES)
        queries.append(both_heads(rot_ref[:, lanes]))
        grads.append(both_heads(grad_ref[:, lanes]))
        product = grad_ref[:, lanes].astype(WIDE) * out_ref[:, lanes].astype(WIDE)
        low = lane_of(product.shape) < HEAD_DIM
        deltas.append(
            jnp.concatenate(
                [
                    jnp.sum(jnp.where(low, product, 0.0), 1, keepdims=True),
                    jnp.sum(jnp.where(low, 0.0, product), 1, keepdims=True),
                ],
                0,
            )
        )
        lses.append(
            jnp.concatenate(
                [lse_ref[:, 2 * p : 2 * p + 1], lse_ref[:, 2 * p + 1 : 2 * p + 2]], 0
            )
        )
    queries_t = [q.T for q in queries]
    grads_t = [g.T for g in grads]

    def one_chunk(c, dq, masked):
        place_c = pl.ds(pl.multiple_of(c * chunk, chunk), chunk)
        keys = keys_ref[place_c, :]
        values = values_ref[place_c, :]
        dk = dkeys[c]
        dv = dvalues[c]
        new = []
        for p in range(pairs):
            weights = jnp.exp(against(queries[p], keys) - lses[p])
            if masked:
                weights = jnp.where(seen(2 * rows, chunk, last_key), weights, 0.0)
            slopes = against(grads[p], values)
            ds = (weights * (slopes - deltas[p])).astype(LOW)
            new.append(dq[p] + multiply(ds, keys))
            dk = dk + multiply(queries_t[p], ds)
            dv = dv + multiply(grads_t[p], weights.astype(LOW))
        dkeys[c] = dk
        dvalues[c] = dv
        return tuple(new)

    start = tuple(jnp.zeros((2 * rows, LANES), WIDE) for _ in range(pairs))
    dq = lax.fori_loop(0, last_chunk, lambda c, d: one_chunk(c, d, False), start)
    dq = one_chunk(last_chunk, dq, True)
    cosine, sine = cosb_ref[...], sinb_ref[...]
    for p in range(pairs):
        pair = one_pair(dq[p]) * scale
        pair = pair * cosine - turned(pair) * sine
        dqkv_ref[here, p * LANES : (p + 1) * LANES] = pair.astype(LOW)

    @pl.when(step == steps - 1)
    def _():
        for c in range(chunks):
            dk, dv = dkeys[c], dvalues[c]
            side = jnp.concatenate(
                [dk[:HEAD_DIM] + dk[HEAD_DIM:], dv[:HEAD_DIM] + dv[HEAD_DIM:]], 0
            )
            flat[c * chunk : (c + 1) * chunk, :] = side.T
        for b in range(keys_ref.shape[0] // rows):
            mine = slice(b * rows, (b + 1) * rows)
            there = pl.ds(pl.multiple_of(order[b] * rows, rows), rows)
            own = flat[there, :]
            back = own * cos_ref[mine, :] - turned(own) * sin_ref[mine, :]
            low = lane_of(own.shape) < HEAD_DIM
            dqkv_ref[mine, pairs * LANES :] = jnp.where(low, back, own).astype(LOW)


def attend(order, qkv, cosine, sine, rows):
    seq, width = qkv.shape[0], qkv.shape[1] - LANES
    pairs = width // LANES
    blocks = seq // rows
    block = lambda w: pl.BlockSpec((rows, w), lambda i, _: (i, 0))
    whole = lambda w, at=0: pl.BlockSpec((seq, w), lambda i, _: (0, at))
    return pl.pallas_call(
        functools.partial(attend_kernel, pairs, 2 * rows),
        grid_spec=pltpu.PrefetchScalarGridSpec(
            num_scalar_prefetch=1,
            grid=(blocks,),
            in_specs=[block(width), whole(LANES, pairs), whole(LANES), whole(LANES), block(LANES), block(LANES)],
            out_specs=[block(width), block(width), whole(LANES), whole(LANES), block(LANES)],
        ),
        out_shape=[
            jax.ShapeDtypeStruct((seq, width), LOW),
            jax.ShapeDtypeStruct((seq, width), LOW),
            jax.ShapeDtypeStruct((seq, LANES), LOW),
            jax.ShapeDtypeStruct((seq, LANES), LOW),
            jax.ShapeDtypeStruct((seq, LANES), WIDE),
        ],
        compiler_params=pltpu.CompilerParams(vmem_limit_bytes=48 << 20),
        cost_estimate=pl.CostEstimate(flops=2 * 2 * seq * seq * width, bytes_accessed=8 << 20, transcendentals=seq * seq * width // HEAD_DIM // 2),
        name="attend",
    )(order, qkv, qkv, cosine, sine, cosine, sine)


def attend_back(order, rotated, grad, out, lse, keys, values, cosine, sine, rows):
    seq, width = rotated.shape
    pairs = width // LANES
    blocks = seq // rows
    block = lambda w: pl.BlockSpec((rows, w), lambda i, _: (i, 0))
    whole = lambda w: pl.BlockSpec((seq, w), lambda i, _: (0, 0))
    chunks = seq // (2 * rows)
    return pl.pallas_call(
        functools.partial(attend_back_kernel, pairs, 2 * rows),
        grid_spec=pltpu.PrefetchScalarGridSpec(
            num_scalar_prefetch=1,
            grid=(blocks,),
            in_specs=[block(width), block(width), block(width), block(LANES), block(LANES), block(LANES),
                      whole(LANES), whole(LANES), whole(LANES), whole(LANES)],
            out_specs=whole(width + LANES),
            scratch_shapes=[
                pltpu.VMEM((chunks, LANES, 2 * rows), WIDE),
                pltpu.VMEM((chunks, LANES, 2 * rows), WIDE),
                pltpu.VMEM((seq, LANES), WIDE),
            ],
        ),
        out_shape=jax.ShapeDtypeStruct((seq, width + LANES), LOW),
        compiler_params=pltpu.CompilerParams(vmem_limit_bytes=48 << 20),
        cost_estimate=pl.CostEstimate(flops=5 * 2 * seq * seq * width, bytes_accessed=8 << 20, transcendentals=seq * seq * width // HEAD_DIM // 2),
        name="attend_back",
    )(order, rotated, grad, out, lse, cosine, sine, keys, values, cosine, sine)


def fold_kernel(count, cuts, qkv_ref, out_ref, joined_ref):
    rows, cut = out_ref.shape[0] // count, out_ref.shape[1] // cuts
    width = qkv_ref.shape[1]
    joined_ref[:, :width] = qkv_ref[...]
    for d in range(count):
        for j in range(cuts):
            there = (d * cuts + j) * rows
            joined_ref[there : there + rows, width:] = out_ref[
                d * rows : (d + 1) * rows, j * cut : (j + 1) * cut
            ]


def fold(qkv, out, count):
    cuts = qkv.shape[0] // out.shape[0]
    width = qkv.shape[1] + out.shape[1] // cuts
    return pl.pallas_call(
        functools.partial(fold_kernel, count, cuts),
        out_shape=jax.ShapeDtypeStruct((qkv.shape[0], width), qkv.dtype),
        compiler_params=pltpu.CompilerParams(vmem_limit_bytes=40 << 20),
        name="fold",
    )(qkv, out)


def unfold_kernel(count, cuts, joined_ref, qkv_ref, out_ref):
    rows, cut = out_ref.shape[0] // count, out_ref.shape[1] // cuts
    width = qkv_ref.shape[1]
    qkv_ref[...] = joined_ref[:, :width]
    for d in range(count):
        for j in range(cuts):
            there = (d * cuts + j) * rows
            out_ref[d * rows : (d + 1) * rows, j * cut : (j + 1) * cut] = joined_ref[
                there : there + rows, width:
            ]


def unfold(joined, cut, cuts, count):
    rows, width = joined.shape
    return pl.pallas_call(
        functools.partial(unfold_kernel, count, cuts),
        out_shape=[
            jax.ShapeDtypeStruct((rows, width - cut), joined.dtype),
            jax.ShapeDtypeStruct((rows // cuts, cut * cuts), joined.dtype),
        ],
        compiler_params=pltpu.CompilerParams(vmem_limit_bytes=40 << 20),
        name="unfold",
    )(joined)


def place_kernel(outer, me_ref, *refs):
    *part_refs, out_ref = refs
    rows = out_ref.shape[2]
    for k, ref in enumerate(part_refs):
        for i in range(outer):
            out_ref[i, me_ref[0] ^ k] = ref[i * rows : (i + 1) * rows, :]


def placed_by_rank(parts, outer):
    rows, width = parts[0].shape[0] // outer, parts[0].shape[1]
    vmem = pl.BlockSpec(memory_space=pltpu.VMEM)
    out = pl.pallas_call(
        functools.partial(place_kernel, outer),
        in_specs=[pl.BlockSpec(memory_space=pltpu.SMEM)] + [vmem] * len(parts),
        out_specs=vmem,
        out_shape=jax.ShapeDtypeStruct((outer, len(parts), rows, width), parts[0].dtype),
        compiler_params=pltpu.CompilerParams(vmem_limit_bytes=40 << 20),
        name="place",
    )(lax.axis_index("ctx").reshape(1), *parts)
    return out.reshape(-1, width)


def spread_kernel(dp_size, chunk, gate_ref, up_ref, out_ref):
    ranks, _, width = out_ref.shape
    for side, ref in enumerate((gate_ref, up_ref)):
        for r in range(ranks):
            for d in range(dp_size):
                here = side * width // 2 + d * chunk
                there = (d * ranks + r) * chunk
                out_ref[r, :, here : here + chunk] = ref[:, there : there + chunk]


def merge_kernel(dp_size, chunk, parts_ref, gate_ref, up_ref):
    ranks, _, width = parts_ref.shape
    for side, ref in enumerate((gate_ref, up_ref)):
        for r in range(ranks):
            for d in range(dp_size):
                here = side * width // 2 + d * chunk
                there = (d * ranks + r) * chunk
                ref[:, there : there + chunk] = parts_ref[r, :, here : here + chunk].astype(WIDE)


def spread(gate, up, dp_size, ctx_size, chunk):
    shape = (ctx_size, gate.shape[0], 2 * dp_size * chunk)
    return pl.pallas_call(
        functools.partial(spread_kernel, dp_size, chunk),
        out_shape=jax.ShapeDtypeStruct(shape, gate.dtype),
        name="spread",
    )(gate, up)


def merge(parts, dp_size, chunk):
    shape = jax.ShapeDtypeStruct((parts.shape[1], parts.shape[0] * dp_size * chunk), WIDE)
    return pl.pallas_call(
        functools.partial(merge_kernel, dp_size, chunk), out_shape=[shape, shape], name="merge"
    )(parts)


def tiles(width, size):
    return [slice(at, min(at + size, width)) for at in range(0, width, size)]


def gate_up_kernel(gate_w_ref, up_w_ref, *refs):
    *piece_refs, gate_ref, up_ref, active_ref, hidden_ref, rows, arrived, left = refs
    copy_out = pltpu.make_async_copy(rows, hidden_ref, left)

    @pl.when(pl.program_id(0) == 0)
    def _():
        copies, at = [], 0
        for k, ref in enumerate(piece_refs):
            here = pl.ds(at, ref.shape[0])
            copies.append(pltpu.make_async_copy(ref, rows.at[here, :], arrived.at[k]))
            copies[-1].start()
            at += ref.shape[0]
        for copy in copies:
            copy.wait()
        copy_out.start()

    width = gate_ref.shape[1]
    sides = jnp.concatenate([gate_w_ref[...], up_w_ref[...]], 1)
    both = multiply(rows[...], sides)
    gate, up = both[:, :width], both[:, width:]
    gate_ref[...] = gate
    up_ref[...] = up
    active_ref[...] = (gate * jax.nn.sigmoid(gate) * up).astype(LOW)

    @pl.when(pl.program_id(0) == pl.num_programs(0) - 1)
    def _():
        copy_out.wait()


def gate_up(pieces, weight):
    depth, width = weight.shape[0], weight.shape[1] // 2
    count = sum(piece.shape[0] for piece in pieces)
    if width % LANES:
        hidden = jnp.concatenate(pieces, 0)
        gate, up = multiply(hidden, weight[:, :width]), multiply(hidden, weight[:, width:])
        return gate, up, (gate * jax.nn.sigmoid(gate) * up).astype(LOW), hidden
    steps = width // LANES
    there = pl.BlockSpec(memory_space=pl.ANY)
    block = pl.BlockSpec((count, LANES), lambda j: (0, j))
    return pl.pallas_call(
        gate_up_kernel,
        grid=(steps,),
        in_specs=[
            pl.BlockSpec((depth, LANES), lambda j: (0, j)),
            pl.BlockSpec((depth, LANES), lambda j: (0, j + steps)),
        ]
        + [there] * len(pieces),
        out_specs=[block, block, block, there],
        out_shape=[
            jax.ShapeDtypeStruct((count, width), WIDE),
            jax.ShapeDtypeStruct((count, width), WIDE),
            jax.ShapeDtypeStruct((count, width), LOW),
            jax.ShapeDtypeStruct((count, depth), LOW),
        ],
        scratch_shapes=[
            pltpu.VMEM((count, depth), LOW),
            pltpu.SemaphoreType.DMA((len(pieces),)),
            pltpu.SemaphoreType.DMA,
        ],
        compiler_params=pltpu.CompilerParams(vmem_limit_bytes=40 << 20),
        cost_estimate=pl.CostEstimate(
            flops=4 * count * depth * width, bytes_accessed=36 << 20, transcendentals=count * width
        ),
        name="gate_up",
    )(weight, weight, *pieces)


def mlp_back_kernel(
    top_ref, gate_ref, up_ref, down_ref, weight_ref, grads_ref, part_ref, down, weight, arrived
):
    width = gate_ref.shape[1]
    first = pl.program_id(0) == 0
    copy_down = pltpu.make_async_copy(down_ref, down, arrived.at[0])
    copy_weight = pltpu.make_async_copy(weight_ref, weight, arrived.at[1])

    @pl.when(first)
    def _():
        copy_down.start()
        copy_weight.start()
        copy_down.wait()

    top = top_ref[...]
    for cut in tiles(width, 2 * LANES):
        shifted = slice(width + cut.start, width + cut.stop)
        slope = against(top, down[cut, :])
        gate, up = gate_ref[:, cut], up_ref[:, cut]
        sigmoid = jax.nn.sigmoid(gate)
        swished = gate * sigmoid
        grads_ref[:, cut] = (slope * up * sigmoid * (1.0 + gate * (1.0 - sigmoid))).astype(LOW)
        grads_ref[:, shifted] = (slope * swished).astype(LOW)

    @pl.when(first)
    def _():
        copy_weight.wait()

    grads = grads_ref[...]
    for cut in tiles(part_ref.shape[1], 2 * LANES):
        part_ref[:, cut] = against(grads, weight[cut, :]).astype(LOW)


def mlp_back(top, gate, up, down, weight, rows):
    count, depth = top.shape
    width = gate.shape[1]
    block = lambda w: pl.BlockSpec((rows, w), lambda i: (i, 0))
    there = pl.BlockSpec(memory_space=pl.ANY)
    return pl.pallas_call(
        mlp_back_kernel,
        grid=(count // rows,),
        in_specs=[block(depth), block(width), block(width), there, there],
        out_specs=[block(2 * width), block(depth)],
        out_shape=[
            jax.ShapeDtypeStruct((count, 2 * width), LOW),
            jax.ShapeDtypeStruct((count, depth), LOW),
        ],
        scratch_shapes=[
            pltpu.VMEM(down.shape, LOW),
            pltpu.VMEM(weight.shape, LOW),
            pltpu.SemaphoreType.DMA((2,)),
        ],
        compiler_params=pltpu.CompilerParams(vmem_limit_bytes=56 << 20),
        cost_estimate=pl.CostEstimate(
            flops=6 * count * depth * width, bytes_accessed=40 << 20, transcendentals=count * width
        ),
        name="mlp_back",
    )(top, gate, up, down, weight)


def out_back_kernel(weight_ref, attn_ref, *refs):
    *piece_refs, grad_ref, sums_ref, rows, arrived = refs
    copies, at = [], 0
    for k, ref in enumerate(piece_refs):
        here = pl.ds(at, ref.shape[0])
        copies.append(pltpu.make_async_copy(ref, rows.at[here, :], arrived.at[k]))
        copies[-1].start()
        at += ref.shape[0]
    turned_attn = attn_ref[...].T
    for copy in copies:
        copy.wait()
    everything = rows[...]
    for cut in tiles(weight_ref.shape[0], 2 * LANES):
        grad_ref[:, cut] = against(everything, weight_ref[cut, :]).astype(LOW)
    for cut in tiles(weight_ref.shape[1], 2 * LANES):
        sums_ref[:, cut] = multiply(turned_attn, rows[:, cut]).astype(LOW)


def out_back(pieces, weight, attn):
    count, width = attn.shape
    depth = weight.shape[1]
    vmem = pl.BlockSpec(memory_space=pltpu.VMEM)
    return pl.pallas_call(
        out_back_kernel,
        in_specs=[vmem, vmem] + [pl.BlockSpec(memory_space=pl.ANY)] * len(pieces),
        out_specs=[vmem, vmem],
        out_shape=[
            jax.ShapeDtypeStruct((count, width), LOW),
            jax.ShapeDtypeStruct((width, depth), LOW),
        ],
        scratch_shapes=[
            pltpu.VMEM((count, depth), LOW),
            pltpu.SemaphoreType.DMA((len(pieces),)),
        ],
        compiler_params=pltpu.CompilerParams(vmem_limit_bytes=48 << 20),
        cost_estimate=pl.CostEstimate(
            flops=4 * count * depth * width, bytes_accessed=16 << 20, transcendentals=0
        ),
        name="out_back",
    )(weight, attn, *pieces)


def norm_scale(values):
    return lax.rsqrt(jnp.mean(values * values, -1, keepdims=True) + NORM_EPS)


def norm_back(grad_hidden, normed, scale_rows, gain):
    gain_grad = jnp.sum(grad_hidden * normed, 0)
    scaled = grad_hidden * gain
    return (
        gain_grad,
        scale_rows * (scaled - normed * jnp.mean(scaled * normed, -1, keepdims=True)),
    )


def split_rows(values, count):
    rows = values.shape[0] // count
    return [values[k * rows : (k + 1) * rows] for k in range(count)]


def local(
    inputs,
    positions,
    block_order,
    norm_attn,
    w_query,
    w_key,
    w_value,
    w_out,
    norm_mlp,
    w_gate,
    w_up,
    w_down,
    cotangent,
):
    row_count = inputs.shape[2]
    model_width = inputs.shape[3]
    block_rows = row_count // 2
    dp_size, ctx_size = lax.axis_size("dp"), lax.axis_size("ctx")
    ctx_rank = lax.axis_index("ctx")
    head_dim = HEAD_DIM
    sharers = ctx_size // KV_HEADS
    query_width = HEADS // ctx_size * head_dim
    qkv_width = query_width + 2 * head_dim
    ff_width = w_gate.shape[1] // ctx_size
    ff_chunk = w_down.shape[0]

    x_low = inputs.reshape(row_count, model_width)
    grad_top = cotangent.reshape(row_count, model_width)
    gain_rows = norm_attn.shape[0]
    own_positions = positions.reshape(gain_rows, -1)
    position_width = own_positions.shape[1]
    own_extras = jnp.concatenate(
        [
            jnp.stack([norm_attn, norm_mlp], 1),
            (own_positions // LANES).astype(LOW),
            (own_positions % LANES).astype(LOW),
        ],
        1,
    )
    own_extras = jnp.pad(own_extras, ((0, 0), (0, LANES - own_extras.shape[1])))

    def pick_attn(rank):
        kv_start = rank // sharers * head_dim
        return jnp.concatenate(
            [
                lax.dynamic_slice_in_dim(w_query, rank * query_width, query_width, 1),
                lax.dynamic_slice_in_dim(w_key, kv_start, head_dim, 1),
                lax.dynamic_slice_in_dim(w_value, kv_start, head_dim, 1),
                own_extras,
            ],
            1,
        )

    cuts = model_width // query_width
    gathered_out = dp_gather(w_out)
    parts_qkv = exchanged(pick_attn)
    parts_qkv, (x_low, columns) = tied_lists(
        parts_qkv, [x_low, spread(w_gate, w_up, dp_size, ctx_size, ff_chunk)]
    )
    block_qkv = jnp.concatenate(in_rank_order(parts_qkv), 0)
    gathered_qkv = dp_gather(block_qkv)
    parts_gate_up = exchanged(
        lambda rank: lax.dynamic_index_in_dim(columns, rank, 0, keepdims=False)
    )
    x_parts, _ = ctx_gather(x_low)
    out_rows = gathered_out.shape[0] // ctx_size
    x_parts, (gathered_out,) = tied_lists(x_parts, [gathered_out])
    parts_out = exchanged(
        lambda rank: lax.dynamic_slice_in_dim(gathered_out, rank * out_rows, out_rows, 0)
    )
    x_all = jnp.concatenate(x_parts, 0)

    sent = block_qkv.reshape(ctx_size, gain_rows, -1)[:, :, qkv_width + 2 :].astype(WIDE)
    sent = LANES * sent[..., :position_width] + sent[..., position_width : 2 * position_width]
    sent = sent.reshape(ctx_size, row_count)
    ranks = [ctx_rank ^ k for k in range(ctx_size)]
    all_positions = jnp.concatenate(
        [lax.dynamic_index_in_dim(sent, r, 0, keepdims=False) for r in ranks]
    )
    frequency = ROPE_BASE ** (-jnp.arange(head_dim // 2, dtype=WIDE) * 2.0 / head_dim)
    angles = all_positions[:, None] * frequency[None, :]
    cosine = jnp.tile(jnp.cos(angles), (1, 4))
    sine = jnp.sin(angles)
    sine = jnp.concatenate([-sine, sine, -sine, sine], 1)
    order = jnp.concatenate([block_order[r] for r in ranks])

    x_wide = x_all.astype(WIDE)
    scale_all = norm_scale(x_wide)
    parts_gate_up, (cosine, sine, scale_all) = tied_lists(parts_gate_up, [cosine, sine, scale_all])
    gathered_qkv, block_gate_up = tied(
        gathered_qkv, jnp.concatenate(in_rank_order(parts_gate_up), 0)
    )
    part_gate_up = dp_gather(block_gate_up)
    part_qkv = gathered_qkv[:, :qkv_width]
    gains = gathered_qkv[:, qkv_width:].astype(WIDE).T
    gain_attn, gain_mlp = gains[0], gains[1]
    normed_attn = x_wide * scale_all
    hidden_attn = (normed_attn * gain_attn).astype(LOW)
    qkv = multiply(hidden_attn, part_qkv)
    x_rows = x_low.astype(WIDE)

    attn_low, rotated, keys, values, log_total = attend(order, qkv, cosine, sine, block_rows)
    (attn_low,), parts_out = tied_lists([attn_low], parts_out)
    part_out = placed_by_rank(parts_out, dp_size // ctx_size)
    mixed, _ = ctx_scatter_sum(multiply(attn_low, part_out).astype(LOW))
    middle = x_rows + mixed
    middle, w_down = tied(middle, w_down)
    part_down = dp_gather(w_down)
    scale_mlp = norm_scale(middle)
    normed_mlp = middle * scale_mlp
    hidden_parts, _ = ctx_gather((normed_mlp * gain_mlp).astype(LOW))
    hidden_parts, (grad_top,) = tied_lists(hidden_parts, [grad_top])
    top_parts, (gate_rows, up_rows, activated, hidden_mlp) = ctx_gather(
        grad_top, gate_up(hidden_parts, part_gate_up)
    )
    top_all = jnp.concatenate(top_parts, 0)
    part_down_w, part_down = tied(outer_sum(activated, top_all).astype(LOW), part_down)
    grad_down = dp_scatter_sum(part_down_w)

    grad_gate_up, part_hidden_mlp = mlp_back(
        top_all, gate_rows, up_rows, part_down, part_gate_up, row_count
    )
    grad_hidden_mlp, (part_gate_up_w,) = ctx_scatter_sum(
        part_hidden_mlp, [outer_sum(hidden_mlp, grad_gate_up).astype(LOW)]
    )
    grad_gate_up_w = dp_scatter_sum(part_gate_up_w)
    gain_mlp_grad, grad_mid_norm = norm_back(grad_hidden_mlp, normed_mlp, scale_mlp, gain_mlp)
    grad_middle = grad_top.astype(WIDE) + grad_mid_norm

    branch_parts, (part_result, grad_down) = ctx_gather(
        grad_middle.astype(LOW), [multiply(activated, part_down).astype(LOW)], [grad_down]
    )
    grad_attn, part_out_w = out_back(branch_parts, part_out, attn_low)
    split_out = part_out_w.reshape(dp_size // ctx_size, ctx_size, -1, model_width)
    parts_out_w = exchanged(
        lambda rank: lax.dynamic_index_in_dim(split_out, rank, 1, keepdims=False)
    )
    grad_attn, part_result = tied(grad_attn, part_result)
    grad_qkv = attend_back(
        order, rotated, grad_attn, attn_low, log_total, keys, values, cosine, sine, block_rows
    )
    part_result, (grad_qkv, *parts_out_w) = ctx_scatter_sum(
        part_result, [grad_qkv], parts_out_w
    )
    part_out_w = jnp.stack(in_rank_order(parts_out_w)).reshape(-1, model_width)
    outputs = (middle + part_result).astype(LOW).reshape(inputs.shape)
    part_hidden_attn = against(grad_qkv, part_qkv)
    gain_attn_grad = jnp.sum(part_hidden_attn * normed_attn, 0)
    gain_grads = jnp.pad(
        jnp.stack([gain_attn_grad, gain_mlp_grad], 1).astype(LOW), ((0, 0), (0, LANES - 2))
    )
    part_qkv_w = jnp.concatenate([outer_sum(hidden_attn, grad_qkv).astype(LOW), gain_grads], 1)
    part_attn_w, part_hidden_attn, outputs = tied(
        fold(part_qkv_w, part_out_w, dp_size), part_hidden_attn.astype(LOW), outputs
    )
    grad_attn_w = dp_scatter_sum(part_attn_w)
    grad_hidden_attn, (grad_gate_up_w,) = ctx_scatter_sum(
        part_hidden_attn, (), [grad_gate_up_w]
    )
    scale_attn = norm_scale(x_rows)
    _, grad_in_norm = norm_back(grad_hidden_attn, x_rows * scale_attn, scale_attn, gain_attn)
    grad_inputs = (grad_middle + grad_in_norm).reshape(inputs.shape)

    gate_up_rows = jnp.stack(columns_to_rows(grad_gate_up_w))
    out_gate, out_up = merge(gate_up_rows, dp_size, ff_chunk)
    out_down = grad_down.astype(WIDE)
    grad_attn_w, out_gate, out_up, grad_inputs = tied(grad_attn_w, out_gate, out_up, grad_inputs)
    grad_qkv_w, grad_out_w = unfold(grad_attn_w, query_width, cuts, 1)
    out_out = grad_out_w.astype(WIDE)
    qkv_rows = columns_to_rows(grad_qkv_w)
    out_query = jnp.concatenate([part[:, :query_width] for part in qkv_rows], 1).astype(WIDE)
    rests = [part[:, query_width:].astype(WIDE) for part in qkv_rows]
    kv_parts = [sum(rests[g * sharers : (g + 1) * sharers]) for g in range(KV_HEADS)]
    out_key = jnp.concatenate([part[:, :head_dim] for part in kv_parts], 1)
    out_value = jnp.concatenate([part[:, head_dim : 2 * head_dim] for part in kv_parts], 1)
    out_gains = sum(rests)[:, 2 * head_dim : 2 * head_dim + 2].T
    return (
        outputs,
        grad_inputs,
        out_gains[0],
        out_query,
        out_key,
        out_value,
        out_out,
        out_gains[1],
        out_gate,
        out_up,
        out_down,
    )


def solution(mesh):
    placed = (
        P("dp", "ctx", None, None),
        P("dp", "ctx", None),
        P(),
        P(("dp", "ctx")),
        P(("dp", "ctx"), None),
        P(("dp", "ctx"), None),
        P(("dp", "ctx"), None),
        P(("dp", "ctx"), None),
        P(("dp", "ctx")),
        P(("dp", "ctx"), None),
        P(("dp", "ctx"), None),
        P(("dp", "ctx"), None),
        P("dp", "ctx", None, None),
    )
    return jax.shard_map(
        local,
        mesh=mesh,
        in_specs=placed,
        out_specs=(
            P("dp", "ctx", None, None),
            P("dp", "ctx", None, None),
            P(("dp", "ctx")),
            P(("dp", "ctx"), None),
            P(("dp", "ctx"), None),
            P(("dp", "ctx"), None),
            P(("dp", "ctx"), None),
            P(("dp", "ctx")),
            P(("dp", "ctx"), None),
            P(("dp", "ctx"), None),
            P(("dp", "ctx"), None),
        ),
        check_vma=False,
    )
```

```python
import functools

import jax
import jax.numpy as jnp
from jax import lax
from jax.experimental import pallas as pl
from jax.experimental.pallas import tpu as pltpu
from jax.sharding import PartitionSpec as P

HEADS = 32
KV_HEADS = 4
HEAD_DIM = 64
LANES = 2 * HEAD_DIM


NORM_EPS = 1e-05
ROPE_BASE = 10000.0
MASKED_SCORE = -1e30
LOW = jnp.bfloat16
WIDE = jnp.float32


def multiply(left, right):
    return jnp.dot(left, right, preferred_element_type=WIDE)


def against(left, right):
    return lax.dot_general(left, right, (((1,), (1,)), ((), ())), preferred_element_type=WIDE)


def outer_sum(left, right):
    return lax.dot_general(left, right, (((0,), (0,)), ((), ())), preferred_element_type=WIDE)


def swapped(block, distance, axis="ctx"):
    route = [(i, i ^ distance) for i in range(lax.axis_size(axis))]
    return lax.ppermute(block, axis, route)


def tied(*values):
    return lax.optimization_barrier(values)


def tied_lists(received, others):
    values = tied(*received, *others)
    return list(values[: len(received)]), list(values[len(received) :])


def ctx_gather(block, first=(), second=()):
    size = lax.axis_size("ctx")
    if size != 4:
        got = [swapped(block, k) for k in range(1, size)]
        second = second(*first) if callable(second) else second
        got, others = tied_lists(got, [*first, *second])
        return [block] + got, others
    top, low = split_rows(block, 2)
    near = [swapped(top, 1), swapped(low, 2)]
    late = [swapped(low, 1), swapped(top, 2)]
    near, first = tied_lists(near, first)
    far = [swapped(near[0], 2), swapped(near[1], 1)]
    second = second(*first) if callable(second) else second
    got, second = tied_lists(late + far, second)
    return [block, near[0], *got[:2], near[1], *got[2:]], first + second


def gather_start(block):
    if lax.axis_size("ctx") != 4:
        return []
    top, low = split_rows(block, 2)
    return [swapped(top, 1), swapped(low, 2)]


def gather_rest(block, near):
    size = lax.axis_size("ctx")
    if size != 4:
        return [swapped(block, k) for k in range(1, size)]
    top, low = split_rows(block, 2)
    return [swapped(near[0], 2), swapped(near[1], 1), swapped(low, 1), swapped(top, 2)]


def gather_end(block, near, rest):
    if lax.axis_size("ctx") != 4:
        return [block, *rest]
    return [block, near[0], rest[2], rest[3], near[1], rest[0], rest[1]]


def ctx_scatter_sum(values, first=(), second=()):
    size = lax.axis_size("ctx")
    parts = split_rows(values, size)
    if size != 4:
        got = [swapped(parts[k].astype(LOW), k) for k in range(1, size)]
        got, others = tied_lists(got, [*first, *second])
        return sum([part.astype(WIDE) for part in got], parts[0].astype(WIDE)), others
    half = parts[0].shape[-1] // 2
    left = [part[:, :half] for part in parts]
    right = [part[:, half:] for part in parts]
    got = [
        swapped(jnp.stack([left[1], left[3]]).astype(LOW), 1),
        swapped(jnp.stack([right[2], right[3]]).astype(LOW), 2),
    ]
    (got_left, got_right), first = tied_lists(got, first)
    got_left, got_right = got_left.astype(WIDE), got_right.astype(WIDE)
    got = [
        swapped((left[2].astype(WIDE) + got_left[1]).astype(LOW), 2),
        swapped((right[1].astype(WIDE) + got_right[1]).astype(LOW), 1),
    ]
    (far_left, far_right), second = tied_lists(got, second)
    total = jnp.concatenate(
        [
            left[0].astype(WIDE) + got_left[0] + far_left.astype(WIDE),
            right[0].astype(WIDE) + got_right[0] + far_right.astype(WIDE),
        ],
        -1,
    )
    return total, first + second


def in_rank_order(parts):
    me = lax.axis_index("ctx")
    stacked = jnp.stack(parts)
    return [
        lax.dynamic_index_in_dim(stacked, me ^ r, 0, keepdims=False) for r in range(len(parts))
    ]


def exchanged(pick):
    me = lax.axis_index("ctx")
    return [pick(me)] + [swapped(pick(me ^ k), k) for k in range(1, lax.axis_size("ctx"))]


def columns_to_rows(block):
    me = lax.axis_index("ctx")
    size = lax.axis_size("ctx")
    rows = block.shape[0] // size
    pieces = [lax.dynamic_slice_in_dim(block, (me ^ k) * rows, rows, 0) for k in range(size)]
    return in_rank_order([pieces[0]] + [swapped(pieces[k], k) for k in range(1, size)])


def dp_gather(block):
    return lax.all_gather(block, "dp", axis=0, tiled=True)


def dp_scatter_sum(block):
    return lax.psum_scatter(block, "dp", scatter_dimension=0, tiled=True)


def lane_of(shape):
    return lax.broadcasted_iota(jnp.int32, shape, 1)


def turned(values):
    first = lane_of(values.shape) % HEAD_DIM < HEAD_DIM // 2
    return jnp.where(
        first,
        pltpu.roll(values, LANES - HEAD_DIM // 2, 1),
        pltpu.roll(values, HEAD_DIM // 2, 1),
    )


def both_heads(pair):
    even = lane_of(pair.shape) < HEAD_DIM
    zero = jnp.zeros_like(pair)
    return jnp.concatenate([jnp.where(even, pair, zero), jnp.where(even, zero, pair)], 0)


def one_pair(stacked):
    rows = stacked.shape[0] // 2
    even = lane_of((rows, LANES)) < HEAD_DIM
    return jnp.where(even, stacked[:rows], stacked[rows:])


def seen(rows, chunk, last_key):
    query = lax.broadcasted_iota(jnp.int32, (rows, chunk), 0) % (chunk // 2)
    key = lax.broadcasted_iota(jnp.int32, (rows, chunk), 1)
    return key <= query + last_key


def attend_kernel(pairs, chunk, order, q_ref, kv_ref, cos_ref, sin_ref, cosb_ref, sinb_ref,
                  out_ref, rot_ref, keys_ref, values_ref, lse_ref):
    rows = chunk // 2
    step = pl.program_id(0)
    chunks = keys_ref.shape[0] // chunk

    @pl.when(step == 0)
    def _():
        for b in range(keys_ref.shape[0] // rows):
            here = slice(b * rows, (b + 1) * rows)
            there = pl.ds(pl.multiple_of(order[b] * rows, rows), rows)
            own = kv_ref[here, :]
            other = pltpu.roll(own, HEAD_DIM, 1)
            low = lane_of(own.shape) < HEAD_DIM
            keys = jnp.where(low, own, other)
            keys = keys * cos_ref[here, :] + turned(keys) * sin_ref[here, :]
            keys_ref[there, :] = keys.astype(LOW)
            values_ref[there, :] = jnp.where(low, other, own).astype(LOW)

    cosine, sine = cosb_ref[...], sinb_ref[...]
    place = order[step]
    last_key = (place % 2) * rows
    for p in range(pairs):
        lanes = slice(p * LANES, (p + 1) * LANES)
        pair = q_ref[:, lanes]
        pair = pair * cosine + turned(pair) * sine
        rot_ref[:, lanes] = (pair.astype(LOW).astype(WIDE) * HEAD_DIM**-0.5).astype(LOW)

    for count in range(1, chunks + 1):

        @pl.when(place // 2 == count - 1)
        def _(count=count):
            visible = seen(2 * rows, chunk, last_key)
            all_lse = jnp.zeros((rows, LANES), WIDE)
            lane = lane_of((rows, LANES))
            for p in range(pairs):
                lanes = slice(p * LANES, (p + 1) * LANES)
                queries = both_heads(rot_ref[:, lanes])
                scores = [
                    against(queries, keys_ref[c * chunk : (c + 1) * chunk, :]) for c in range(count)
                ]
                scores[-1] = jnp.where(visible, scores[-1], MASKED_SCORE)
                top = jnp.max(functools.reduce(jnp.maximum, scores), 1, keepdims=True)
                weights = [jnp.exp(s - top) for s in scores]
                total = jnp.sum(functools.reduce(jnp.add, weights), 1, keepdims=True)
                mixture = sum(
                    multiply(w.astype(LOW), values_ref[c * chunk : (c + 1) * chunk, :])
                    for c, w in enumerate(weights)
                )
                out_ref[:, lanes] = one_pair(mixture / total).astype(LOW)
                lse = top + jnp.log(total)
                all_lse = jnp.where(lane == 2 * p, lse[:rows], all_lse)
                all_lse = jnp.where(lane == 2 * p + 1, lse[rows:], all_lse)
            lse_ref[...] = all_lse


def attend_back_kernel(pairs, chunk, order, rot_ref, grad_ref, out_ref, lse_ref, cosb_ref, sinb_ref,
                       keys_ref, values_ref, cos_ref, sin_ref, dqkv_ref, dkeys, dvalues, flat):
    rows = chunk // 2
    step = pl.program_id(0)
    steps = pl.num_programs(0)
    chunks = keys_ref.shape[0] // chunk
    scale = HEAD_DIM**-0.5

    @pl.when(step == 0)
    def _():
        dkeys[...] = jnp.zeros_like(dkeys)
        dvalues[...] = jnp.zeros_like(dvalues)

    place = order[step]
    last_chunk = place // 2
    last_key = (place % 2) * rows
    here = pl.ds(pl.multiple_of(step * rows, rows), rows)
    queries, grads, lses, deltas = [], [], [], []
    for p in range(pairs):
        lanes = slice(p * LANES, (p + 1) * LANES)
        queries.append(both_heads(rot_ref[:, lanes]))
        grads.append(both_heads(grad_ref[:, lanes]))
        product = grad_ref[:, lanes].astype(WIDE) * out_ref[:, lanes].astype(WIDE)
        low = lane_of(product.shape) < HEAD_DIM
        deltas.append(
            jnp.concatenate(
                [
                    jnp.sum(jnp.where(low, product, 0.0), 1, keepdims=True),
                    jnp.sum(jnp.where(low, 0.0, product), 1, keepdims=True),
                ],
                0,
            )
        )
        lses.append(
            jnp.concatenate(
                [lse_ref[:, 2 * p : 2 * p + 1], lse_ref[:, 2 * p + 1 : 2 * p + 2]], 0
            )
        )
    queries_t = [q.T for q in queries]
    grads_t = [g.T for g in grads]

    cosine, sine = cosb_ref[...], sinb_ref[...]
    for count in range(1, chunks + 1):

        @pl.when(last_chunk == count - 1)
        def _(count=count):
            visible = seen(2 * rows, chunk, last_key)
            for p in range(pairs):
                dq = None
                for c in range(count):
                    place_c = slice(c * chunk, (c + 1) * chunk)
                    keys = keys_ref[place_c, :]
                    values = values_ref[place_c, :]
                    weights = jnp.exp(against(queries[p], keys) - lses[p])
                    if c == count - 1:
                        weights = jnp.where(visible, weights, 0.0)
                    slopes = against(grads[p], values)
                    ds = (weights * (slopes - deltas[p])).astype(LOW)
                    part = multiply(ds, keys)
                    dq = part if dq is None else dq + part
                    dkeys[c] += multiply(queries_t[p], ds)
                    dvalues[c] += multiply(grads_t[p], weights.astype(LOW))
                pair = one_pair(dq) * scale
                pair = pair * cosine - turned(pair) * sine
                dqkv_ref[here, p * LANES : (p + 1) * LANES] = pair.astype(LOW)

    @pl.when(step == steps - 1)
    def _():
        for c in range(chunks):
            dk, dv = dkeys[c], dvalues[c]
            side = jnp.concatenate(
                [dk[:HEAD_DIM] + dk[HEAD_DIM:], dv[:HEAD_DIM] + dv[HEAD_DIM:]], 0
            )
            flat[c * chunk : (c + 1) * chunk, :] = side.T
        for b in range(keys_ref.shape[0] // rows):
            mine = slice(b * rows, (b + 1) * rows)
            there = pl.ds(pl.multiple_of(order[b] * rows, rows), rows)
            own = flat[there, :]
            back = own * cos_ref[mine, :] - turned(own) * sin_ref[mine, :]
            low = lane_of(own.shape) < HEAD_DIM
            dqkv_ref[mine, pairs * LANES :] = jnp.where(low, back, own).astype(LOW)


def attend(order, qkv, cosine, sine, rows):
    seq, width = qkv.shape[0], qkv.shape[1] - LANES
    pairs = width // LANES
    blocks = seq // rows
    block = lambda w: pl.BlockSpec((rows, w), lambda i, _: (i, 0))
    whole = lambda w, at=0: pl.BlockSpec((seq, w), lambda i, _: (0, at))
    return pl.pallas_call(
        functools.partial(attend_kernel, pairs, 2 * rows),
        grid_spec=pltpu.PrefetchScalarGridSpec(
            num_scalar_prefetch=1,
            grid=(blocks,),
            in_specs=[block(width), whole(LANES, pairs), whole(LANES), whole(LANES), block(LANES), block(LANES)],
            out_specs=[block(width), block(width), whole(LANES), whole(LANES), block(LANES)],
        ),
        out_shape=[
            jax.ShapeDtypeStruct((seq, width), LOW),
            jax.ShapeDtypeStruct((seq, width), LOW),
            jax.ShapeDtypeStruct((seq, LANES), LOW),
            jax.ShapeDtypeStruct((seq, LANES), LOW),
            jax.ShapeDtypeStruct((seq, LANES), WIDE),
        ],
        compiler_params=pltpu.CompilerParams(vmem_limit_bytes=60 << 20),
        cost_estimate=pl.CostEstimate(flops=2 * 2 * seq * seq * width, bytes_accessed=8 << 20, transcendentals=seq * seq * width // HEAD_DIM // 2),
        name="attend",
    )(order, qkv, qkv, cosine, sine, cosine, sine)


def attend_back(order, rotated, grad, out, lse, keys, values, cosine, sine, rows):
    seq, width = rotated.shape
    pairs = width // LANES
    blocks = seq // rows
    block = lambda w: pl.BlockSpec((rows, w), lambda i, _: (i, 0))
    whole = lambda w: pl.BlockSpec((seq, w), lambda i, _: (0, 0))
    chunks = seq // (2 * rows)
    return pl.pallas_call(
        functools.partial(attend_back_kernel, pairs, 2 * rows),
        grid_spec=pltpu.PrefetchScalarGridSpec(
            num_scalar_prefetch=1,
            grid=(blocks,),
            in_specs=[block(width), block(width), block(width), block(LANES), block(LANES), block(LANES),
                      whole(LANES), whole(LANES), whole(LANES), whole(LANES)],
            out_specs=whole(width + LANES),
            scratch_shapes=[
                pltpu.VMEM((chunks, LANES, 2 * rows), WIDE),
                pltpu.VMEM((chunks, LANES, 2 * rows), WIDE),
                pltpu.VMEM((seq, LANES), WIDE),
            ],
        ),
        out_shape=jax.ShapeDtypeStruct((seq, width + LANES), LOW),
        compiler_params=pltpu.CompilerParams(vmem_limit_bytes=60 << 20),
        cost_estimate=pl.CostEstimate(flops=5 * 2 * seq * seq * width, bytes_accessed=8 << 20, transcendentals=seq * seq * width // HEAD_DIM // 2),
        name="attend_back",
    )(order, rotated, grad, out, lse, cosine, sine, keys, values, cosine, sine)


def attn_sums_kernel(count, me_ref, hidden_ref, grad_ref, weight_ref, slopes_ref, *refs):
    *out_refs, joined_ref = refs
    outer, chunk = count // len(out_refs), joined_ref.shape[0] // count
    rows = out_refs[0].shape[0] // outer
    cuts = chunk // rows
    cut = out_refs[0].shape[1] // cuts
    width = grad_ref.shape[1]
    for k, ref in enumerate(out_refs):
        for i in range(outer):
            block = (me_ref[0] ^ k) * outer + i
            for j in range(cuts):
                there = pl.ds(pl.multiple_of(block * chunk, chunk) + j * rows, rows)
                joined_ref[there, width + LANES :] = ref[
                    i * rows : (i + 1) * rows, j * cut : (j + 1) * cut
                ]
    grad = grad_ref[...]
    lane = lane_of((chunk, LANES))
    for d in range(count):
        here = slice(d * chunk, (d + 1) * chunk)
        sums = lax.dot_general(
            hidden_ref[:, here], grad, (((0,), (0,)), ((), ())), preferred_element_type=WIDE
        )
        joined_ref[here, :width] = sums.astype(LOW)
        gain = weight_ref[here, width:].astype(WIDE)[:, :1]
        slope = jnp.sum(sums * weight_ref[here, :width].astype(WIDE), 1, keepdims=True) / gain
        both = jnp.where(lane == 0, slope, slopes_ref[here, :])
        joined_ref[here, width : width + LANES] = both.astype(LOW)


def attn_sums(hidden, grad, weight, slopes, parts, count):
    depth, width = hidden.shape[1], grad.shape[1]
    total = sum(part.shape[0] for part in parts)
    full = width + LANES + parts[0].shape[1] * total // depth
    vmem = pl.BlockSpec(memory_space=pltpu.VMEM)
    return pl.pallas_call(
        functools.partial(attn_sums_kernel, count),
        in_specs=[pl.BlockSpec(memory_space=pltpu.SMEM)] + [vmem] * (4 + len(parts)),
        out_specs=vmem,
        out_shape=jax.ShapeDtypeStruct((depth, full), LOW),
        compiler_params=pltpu.CompilerParams(vmem_limit_bytes=60 << 20),
        cost_estimate=pl.CostEstimate(
            flops=2 * hidden.shape[0] * depth * width, bytes_accessed=16 << 20, transcendentals=0
        ),
        name="attn_sums",
    )(lax.axis_index("ctx").reshape(1), hidden, grad, weight, slopes, *parts)


def finish_kernel(sharers, me_ref, joined_ref, *refs):
    *part_refs, query_ref, key_ref, value_ref, out_ref, gains_ref = refs
    ranks = len(part_refs)
    rows, full = part_refs[0].shape
    width = full - LANES
    query_width = query_ref.shape[1] // ranks
    head_dim = (width - query_width) // 2
    for k, ref in enumerate(part_refs):
        there = pl.ds(pl.multiple_of((me_ref[0] ^ k) * query_width, query_width), query_width)
        query_ref[:, there] = ref[:, :query_width].astype(WIDE)
    rests = [ref[:, query_width:width].astype(WIDE) for ref in part_refs]
    gains_ref[...] = sum(ref[:, width:].astype(WIDE) for ref in part_refs)
    for group in range(ranks // sharers):
        total = jnp.zeros((rows, 2 * head_dim), WIDE)
        for k, rest in enumerate(rests):
            total = total + jnp.where((me_ref[0] ^ k) // sharers == group, rest, 0.0)
        here = slice(group * head_dim, (group + 1) * head_dim)
        key_ref[:, here] = total[:, :head_dim]
        value_ref[:, here] = total[:, head_dim:]
    cut = joined_ref.shape[1] - full
    for j in range(out_ref.shape[1] // cut):
        out_ref[:, j * cut : (j + 1) * cut] = joined_ref[
            j * rows : (j + 1) * rows, full:
        ].astype(WIDE)


def finish(joined, parts, sharers):
    ranks, rows = len(parts), parts[0].shape[0]
    depth = joined.shape[0] // rows * (joined.shape[1] - parts[0].shape[1])
    head_dim = HEAD_DIM
    query_width = parts[0].shape[1] - 2 * head_dim - LANES
    vmem = pl.BlockSpec(memory_space=pltpu.VMEM)
    widths = [ranks * query_width] + [ranks // sharers * head_dim] * 2 + [depth, LANES]
    return pl.pallas_call(
        functools.partial(finish_kernel, sharers),
        in_specs=[pl.BlockSpec(memory_space=pltpu.SMEM)] + [vmem] * (1 + ranks),
        out_specs=[vmem] * 5,
        out_shape=[jax.ShapeDtypeStruct((rows, width), WIDE) for width in widths],
        name="finish",
    )(lax.axis_index("ctx").reshape(1), joined, *parts)


def place_kernel(outer, me_ref, *refs):
    *part_refs, out_ref, arrived = refs
    rows = out_ref.shape[2]
    copies = [
        pltpu.make_async_copy(
            ref.at[pl.ds(i * rows, rows), :],
            out_ref.at[i, me_ref[0] ^ k],
            arrived.at[k * outer + i],
        )
        for k, ref in enumerate(part_refs)
        for i in range(outer)
    ]
    for copy in copies:
        copy.start()
    for copy in copies:
        copy.wait()


def placed_by_rank(parts, outer):
    rows, width = parts[0].shape[0] // outer, parts[0].shape[1]
    out = pl.pallas_call(
        functools.partial(place_kernel, outer),
        in_specs=[pl.BlockSpec(memory_space=pltpu.SMEM)]
        + [pl.BlockSpec(memory_space=pltpu.HBM)] * len(parts),
        out_specs=pl.BlockSpec(memory_space=pltpu.VMEM),
        out_shape=jax.ShapeDtypeStruct((outer, len(parts), rows, width), parts[0].dtype),
        scratch_shapes=[pltpu.SemaphoreType.DMA((outer * len(parts),))],
        compiler_params=pltpu.CompilerParams(vmem_limit_bytes=40 << 20),
        name="place",
    )(lax.axis_index("ctx").reshape(1), *parts)
    return out.reshape(-1, width)


def spread_kernel(dp_size, chunk, gate_ref, up_ref, out_ref):
    ranks, _, width = out_ref.shape
    for side, ref in enumerate((gate_ref, up_ref)):
        for r in range(ranks):
            for d in range(dp_size):
                here = side * width // 2 + d * chunk
                there = (d * ranks + r) * chunk
                out_ref[r, :, here : here + chunk] = ref[:, there : there + chunk]


def merge_kernel(dp_size, chunk, parts_ref, gate_ref, up_ref):
    ranks, _, width = parts_ref.shape
    for side, ref in enumerate((gate_ref, up_ref)):
        for r in range(ranks):
            for d in range(dp_size):
                here = side * width // 2 + d * chunk
                there = (d * ranks + r) * chunk
                ref[:, there : there + chunk] = parts_ref[r, :, here : here + chunk].astype(WIDE)


def spread(gate, up, dp_size, ctx_size, chunk):
    shape = (ctx_size, gate.shape[0], 2 * dp_size * chunk)
    return pl.pallas_call(
        functools.partial(spread_kernel, dp_size, chunk),
        out_shape=jax.ShapeDtypeStruct(shape, gate.dtype),
        name="spread",
    )(gate, up)


def merge(parts, dp_size, chunk):
    shape = jax.ShapeDtypeStruct((parts.shape[1], parts.shape[0] * dp_size * chunk), WIDE)
    return pl.pallas_call(
        functools.partial(merge_kernel, dp_size, chunk), out_shape=[shape, shape], name="merge"
    )(parts)


def tiles(width, size):
    return [slice(at, min(at + size, width)) for at in range(0, width, size)]


def gate_up_kernel(gate_w_ref, up_w_ref, *refs):
    *piece_refs, gate_ref, up_ref, active_ref, hidden_ref, rows, arrived, left = refs
    copy_out = pltpu.make_async_copy(rows, hidden_ref, left)

    @pl.when(pl.program_id(0) == 0)
    def _():
        copies, at = [], 0
        for k, ref in enumerate(piece_refs):
            here = pl.ds(at, ref.shape[0])
            copies.append(pltpu.make_async_copy(ref, rows.at[here, :], arrived.at[k]))
            copies[-1].start()
            at += ref.shape[0]
        for copy in copies:
            copy.wait()
        copy_out.start()

    width = gate_ref.shape[1]
    sides = jnp.concatenate([gate_w_ref[...], up_w_ref[...]], 1)
    both = multiply(rows[...], sides)
    gate, up = both[:, :width], both[:, width:]
    gate_ref[...] = gate
    up_ref[...] = up
    active_ref[...] = (gate * jax.nn.sigmoid(gate) * up).astype(LOW)

    @pl.when(pl.program_id(0) == pl.num_programs(0) - 1)
    def _():
        copy_out.wait()


def gate_up(pieces, weight):
    depth, width = weight.shape[0], weight.shape[1] // 2
    count = sum(piece.shape[0] for piece in pieces)
    if width % LANES:
        hidden = jnp.concatenate(pieces, 0)
        gate, up = multiply(hidden, weight[:, :width]), multiply(hidden, weight[:, width:])
        return gate, up, (gate * jax.nn.sigmoid(gate) * up).astype(LOW), hidden
    steps = width // LANES
    there = pl.BlockSpec(memory_space=pl.ANY)
    block = pl.BlockSpec((count, LANES), lambda j: (0, j))
    return pl.pallas_call(
        gate_up_kernel,
        grid=(steps,),
        in_specs=[
            pl.BlockSpec((depth, LANES), lambda j: (0, j)),
            pl.BlockSpec((depth, LANES), lambda j: (0, j + steps)),
        ]
        + [pl.BlockSpec(memory_space=pltpu.HBM)] * len(pieces),
        out_specs=[block, block, block, there],
        out_shape=[
            jax.ShapeDtypeStruct((count, width), WIDE),
            jax.ShapeDtypeStruct((count, width), WIDE),
            jax.ShapeDtypeStruct((count, width), LOW),
            jax.ShapeDtypeStruct((count, depth), LOW),
        ],
        scratch_shapes=[
            pltpu.VMEM((count, depth), LOW),
            pltpu.SemaphoreType.DMA((len(pieces),)),
            pltpu.SemaphoreType.DMA,
        ],
        compiler_params=pltpu.CompilerParams(vmem_limit_bytes=60 << 20),
        cost_estimate=pl.CostEstimate(
            flops=4 * count * depth * width, bytes_accessed=36 << 20, transcendentals=count * width
        ),
        name="gate_up",
    )(weight, weight, *pieces)


def down_sums_kernel(active_ref, *refs):
    *piece_refs, sums_ref, rows_ref, arrived = refs
    copies, at = [], 0
    for k, ref in enumerate(piece_refs):
        here = pl.ds(at, ref.shape[0])
        copies.append(pltpu.make_async_copy(ref, rows_ref.at[here, :], arrived.at[k]))
        copies[-1].start()
        at += ref.shape[0]
    turned_active = active_ref[...].T
    for copy in copies:
        copy.wait()
    for cut in tiles(sums_ref.shape[1], 2 * LANES):
        sums_ref[:, cut] = multiply(turned_active, rows_ref[:, cut]).astype(LOW)


def down_sums(active, pieces):
    count, width = active.shape
    depth = pieces[0].shape[1]
    vmem = pl.BlockSpec(memory_space=pltpu.VMEM)
    return pl.pallas_call(
        down_sums_kernel,
        in_specs=[vmem] + [pl.BlockSpec(memory_space=pl.ANY)] * len(pieces),
        out_specs=[vmem, vmem],
        out_shape=[
            jax.ShapeDtypeStruct((width, depth), LOW),
            jax.ShapeDtypeStruct((count, depth), LOW),
        ],
        scratch_shapes=[pltpu.SemaphoreType.DMA((len(pieces),))],
        compiler_params=pltpu.CompilerParams(vmem_limit_bytes=60 << 20),
        cost_estimate=pl.CostEstimate(
            flops=2 * count * depth * width, bytes_accessed=18 << 20, transcendentals=0
        ),
        name="down_sums",
    )(active, *pieces)


def mlp_back_kernel(
    top_ref, gate_ref, up_ref, down_ref, weight_ref, grads_ref, part_ref, down, weight, arrived
):
    width = gate_ref.shape[1]
    first = pl.program_id(0) == 0
    copy_down = pltpu.make_async_copy(down_ref, down, arrived.at[0])
    copy_weight = pltpu.make_async_copy(weight_ref, weight, arrived.at[1])

    @pl.when(first)
    def _():
        copy_down.start()
        copy_weight.start()
        copy_down.wait()

    top = top_ref[...]
    for cut in tiles(width, 2 * LANES):
        shifted = slice(width + cut.start, width + cut.stop)
        slope = against(top, down[cut, :])
        gate, up = gate_ref[:, cut], up_ref[:, cut]
        sigmoid = jax.nn.sigmoid(gate)
        swished = gate * sigmoid
        grads_ref[:, cut] = (slope * up * sigmoid * (1.0 + gate * (1.0 - sigmoid))).astype(LOW)
        grads_ref[:, shifted] = (slope * swished).astype(LOW)

    @pl.when(first)
    def _():
        copy_weight.wait()

    grads = grads_ref[...]
    for cut in tiles(part_ref.shape[1], 2 * LANES):
        part_ref[:, cut] = against(grads, weight[cut, :]).astype(LOW)


def mlp_back(top, gate, up, down, weight, rows):
    count, depth = top.shape
    width = gate.shape[1]
    block = lambda w: pl.BlockSpec((rows, w), lambda i: (i, 0))
    there = pl.BlockSpec(memory_space=pl.ANY)
    return pl.pallas_call(
        mlp_back_kernel,
        grid=(count // rows,),
        in_specs=[block(depth), block(width), block(width), there, there],
        out_specs=[block(2 * width), block(depth)],
        out_shape=[
            jax.ShapeDtypeStruct((count, 2 * width), LOW),
            jax.ShapeDtypeStruct((count, depth), LOW),
        ],
        scratch_shapes=[
            pltpu.VMEM(down.shape, LOW),
            pltpu.VMEM(weight.shape, LOW),
            pltpu.SemaphoreType.DMA((2,)),
        ],
        compiler_params=pltpu.CompilerParams(vmem_limit_bytes=60 << 20),
        cost_estimate=pl.CostEstimate(
            flops=6 * count * depth * width, bytes_accessed=40 << 20, transcendentals=count * width
        ),
        name="mlp_back",
    )(top, gate, up, down, weight)


def out_back_kernel(weight_ref, attn_ref, *refs):
    *piece_refs, grad_ref, sums_ref, rows, arrived = refs
    copies, at = [], 0
    for k, ref in enumerate(piece_refs):
        here = pl.ds(at, ref.shape[0])
        copies.append(pltpu.make_async_copy(ref, rows.at[here, :], arrived.at[k]))
        copies[-1].start()
        at += ref.shape[0]
    turned_attn = attn_ref[...].T
    for copy in copies:
        copy.wait()
    everything = rows[...]
    for cut in tiles(weight_ref.shape[0], 2 * LANES):
        grad_ref[:, cut] = against(everything, weight_ref[cut, :]).astype(LOW)
    for cut in tiles(weight_ref.shape[1], 2 * LANES):
        sums_ref[:, cut] = multiply(turned_attn, rows[:, cut]).astype(LOW)


def out_back(pieces, weight, attn):
    count, width = attn.shape
    depth = weight.shape[1]
    vmem = pl.BlockSpec(memory_space=pltpu.VMEM)
    return pl.pallas_call(
        out_back_kernel,
        in_specs=[vmem, vmem] + [pl.BlockSpec(memory_space=pltpu.HBM)] * len(pieces),
        out_specs=[vmem, vmem],
        out_shape=[
            jax.ShapeDtypeStruct((count, width), LOW),
            jax.ShapeDtypeStruct((width, depth), LOW),
        ],
        scratch_shapes=[
            pltpu.VMEM((count, depth), LOW),
            pltpu.SemaphoreType.DMA((len(pieces),)),
        ],
        compiler_params=pltpu.CompilerParams(vmem_limit_bytes=60 << 20),
        cost_estimate=pl.CostEstimate(
            flops=4 * count * depth * width, bytes_accessed=16 << 20, transcendentals=0
        ),
        name="out_back",
    )(weight, attn, *pieces)


def norm_scale(values):
    return lax.rsqrt(jnp.mean(values * values, -1, keepdims=True) + NORM_EPS)


def norm_back(grad_hidden, normed, scale_rows, gain):
    gain_grad = jnp.sum(grad_hidden * normed, 0)
    scaled = grad_hidden * gain
    return (
        gain_grad,
        scale_rows * (scaled - normed * jnp.mean(scaled * normed, -1, keepdims=True)),
    )


def join_kernel(me_ref, *refs):
    *block_refs, out_ref = refs
    count = len(block_refs) // 2
    for k in range(count):
        out_ref[me_ref[0] ^ (2 * k)] = block_refs[k][...]
        out_ref[me_ref[0] ^ (2 * k + 1)] = block_refs[count + k][...]


def dp_blocks(block):
    return [block] + [swapped(block, 2 * k, "dp") for k in range(1, lax.axis_size("dp") // 2)]


def dp_joined(blocks):
    rows, width = blocks[0].shape
    count = 2 * len(blocks)
    others = [swapped(block, 1, "dp") for block in blocks]
    vmem = pl.BlockSpec(memory_space=pltpu.VMEM)
    out = pl.pallas_call(
        join_kernel,
        in_specs=[pl.BlockSpec(memory_space=pltpu.SMEM)] + [vmem] * count,
        out_specs=vmem,
        out_shape=jax.ShapeDtypeStruct((count, rows, width), blocks[0].dtype),
        compiler_params=pltpu.CompilerParams(vmem_limit_bytes=40 << 20),
        name="join",
    )(lax.axis_index("dp").reshape(1), *blocks, *others)
    return out.reshape(count * rows, width)


def split_rows(values, count):
    rows = values.shape[0] // count
    return [values[k * rows : (k + 1) * rows] for k in range(count)]


def local(
    inputs,
    positions,
    block_order,
    norm_attn,
    w_query,
    w_key,
    w_value,
    w_out,
    norm_mlp,
    w_gate,
    w_up,
    w_down,
    cotangent,
):
    row_count = inputs.shape[2]
    model_width = inputs.shape[3]
    block_rows = row_count // 2
    dp_size, ctx_size = lax.axis_size("dp"), lax.axis_size("ctx")
    ctx_rank = lax.axis_index("ctx")
    head_dim = HEAD_DIM
    sharers = ctx_size // KV_HEADS
    query_width = HEADS // ctx_size * head_dim
    qkv_width = query_width + 2 * head_dim
    ff_width = w_gate.shape[1] // ctx_size
    ff_chunk = w_down.shape[0]

    x_low = inputs.reshape(row_count, model_width)
    grad_top = cotangent.reshape(row_count, model_width)
    gain_rows = norm_attn.shape[0]
    own_positions = positions.reshape(gain_rows, -1)
    position_width = own_positions.shape[1]
    own_extras = jnp.concatenate(
        [
            jnp.stack([norm_attn, norm_mlp], 1),
            (own_positions // LANES).astype(LOW),
            (own_positions % LANES).astype(LOW),
        ],
        1,
    )
    own_extras = jnp.pad(own_extras, ((0, 0), (0, LANES - own_extras.shape[1])))

    def pick_attn(rank):
        kv_start = rank // sharers * head_dim
        return jnp.concatenate(
            [
                lax.dynamic_slice_in_dim(w_query, rank * query_width, query_width, 1),
                lax.dynamic_slice_in_dim(w_key, kv_start, head_dim, 1),
                lax.dynamic_slice_in_dim(w_value, kv_start, head_dim, 1),
                own_extras,
            ],
            1,
        )

    cuts = model_width // query_width
    blocks_out = dp_blocks(w_out)
    parts_qkv = exchanged(pick_attn)
    parts_qkv, (x_low, columns) = tied_lists(
        parts_qkv, [x_low, spread(w_gate, w_up, dp_size, ctx_size, ff_chunk)]
    )
    block_qkv = jnp.concatenate(in_rank_order(parts_qkv), 0)
    gathered_qkv = dp_gather(block_qkv)
    parts_gate_up = exchanged(
        lambda rank: lax.dynamic_index_in_dim(columns, rank, 0, keepdims=False)
    )
    x_parts, (block_gate_up,) = ctx_gather(
        x_low, [jnp.concatenate(in_rank_order(parts_gate_up), 0)]
    )
    part_gate_up = dp_gather(block_gate_up)
    x_parts[-1], grad_top = tied(x_parts[-1], grad_top)
    near = gather_start(grad_top)
    x_all = jnp.concatenate(x_parts, 0)

    sent = block_qkv.reshape(ctx_size, gain_rows, -1)[:, :, qkv_width + 2 :].astype(WIDE)
    sent = LANES * sent[..., :position_width] + sent[..., position_width : 2 * position_width]
    sent = sent.reshape(ctx_size, row_count)
    ranks = [ctx_rank ^ k for k in range(ctx_size)]
    all_positions = jnp.concatenate(
        [lax.dynamic_index_in_dim(sent, r, 0, keepdims=False) for r in ranks]
    )
    frequency = ROPE_BASE ** (-jnp.arange(head_dim // 2, dtype=WIDE) * 2.0 / head_dim)
    angles = all_positions[:, None] * frequency[None, :]
    cosine = jnp.tile(jnp.cos(angles), (1, 4))
    sine = jnp.sin(angles)
    sine = jnp.concatenate([-sine, sine, -sine, sine], 1)
    order = jnp.concatenate([block_order[r] for r in ranks])

    x_wide = x_all.astype(WIDE)
    scale_all = norm_scale(x_wide)
    (gathered_qkv, cosine, sine, scale_all), waited = tied_lists(
        [gathered_qkv, cosine, sine, scale_all], [*blocks_out, *near]
    )
    blocks_out, near = waited[: len(blocks_out)], waited[len(blocks_out) :]
    gathered_out = dp_joined(blocks_out)
    out_rows = gathered_out.shape[0] // ctx_size
    parts_out = exchanged(
        lambda rank: lax.dynamic_slice_in_dim(gathered_out, rank * out_rows, out_rows, 0)
    )
    part_qkv = gathered_qkv[:, :qkv_width]
    gains = gathered_qkv[:, qkv_width:].astype(WIDE).T
    gain_attn, gain_mlp = gains[0], gains[1]
    normed_attn = x_wide * scale_all
    hidden_attn = (normed_attn * gain_attn).astype(LOW)
    qkv = multiply(hidden_attn, part_qkv)
    x_rows = x_low.astype(WIDE)

    attn_low, rotated, keys, values, log_total = attend(order, qkv, cosine, sine, block_rows)
    (attn_low,), parts_out = tied_lists([attn_low], parts_out)
    part_out = placed_by_rank(parts_out, dp_size // ctx_size)
    mixed, _ = ctx_scatter_sum(multiply(attn_low, part_out).astype(LOW))
    middle = x_rows + mixed
    middle, w_down = tied(middle, w_down)
    part_down = dp_gather(w_down)
    scale_mlp = norm_scale(middle)
    normed_mlp = middle * scale_mlp
    hidden_parts, _ = ctx_gather((normed_mlp * gain_mlp).astype(LOW))
    hidden_parts[2], grad_top, *near = tied(hidden_parts[2], grad_top, *near)
    rest = gather_rest(grad_top, near)
    rest, (gate_rows, up_rows, activated, hidden_mlp) = tied_lists(
        rest, gate_up(hidden_parts, part_gate_up)
    )
    top_parts = gather_end(grad_top, near, rest)
    part_down_w, top_all = down_sums(activated, top_parts)
    part_down_w, part_down = tied(part_down_w, part_down)
    grad_down = dp_scatter_sum(part_down_w)

    grad_gate_up, part_hidden_mlp = mlp_back(
        top_all, gate_rows, up_rows, part_down, part_gate_up, row_count
    )
    grad_hidden_mlp, (part_gate_up_w,) = ctx_scatter_sum(
        part_hidden_mlp, [outer_sum(hidden_mlp, grad_gate_up).astype(LOW)]
    )
    grad_gate_up_w = dp_scatter_sum(part_gate_up_w)
    gain_mlp_grad, grad_mid_norm = norm_back(grad_hidden_mlp, normed_mlp, scale_mlp, gain_mlp)
    grad_middle = grad_top.astype(WIDE) + grad_mid_norm

    branch_parts, (part_result, grad_down) = ctx_gather(
        grad_middle.astype(LOW), [multiply(activated, part_down).astype(LOW)], [grad_down]
    )
    branch_parts, (part_result,) = tied_lists(branch_parts, [part_result])
    grad_attn, part_out_w = out_back(branch_parts, part_out, attn_low)
    split_out = part_out_w.reshape(dp_size // ctx_size, ctx_size, -1, model_width)
    parts_out_w = exchanged(
        lambda rank: lax.dynamic_index_in_dim(split_out, rank, 1, False).reshape(-1, model_width)
    )
    grad_qkv = attend_back(
        order, rotated, grad_attn, attn_low, log_total, keys, values, cosine, sine, block_rows
    )
    part_result, (grad_qkv, *parts_out_w) = ctx_scatter_sum(
        part_result, [grad_qkv, *parts_out_w]
    )
    outputs = (middle + part_result).astype(LOW).reshape(inputs.shape)
    slopes = jnp.pad(gain_mlp_grad[:, None], ((0, 0), (1, LANES - 2)))
    part_attn_w = attn_sums(hidden_attn, grad_qkv, gathered_qkv, slopes, parts_out_w, dp_size)
    grad_hidden_attn, (part_attn_w, grad_gate_up_w) = ctx_scatter_sum(
        against(grad_qkv, part_qkv).astype(LOW), [part_attn_w], [grad_gate_up_w]
    )
    grad_attn_w = dp_scatter_sum(part_attn_w)
    scale_attn = norm_scale(x_rows)
    _, grad_in_norm = norm_back(grad_hidden_attn, x_rows * scale_attn, scale_attn, gain_attn)
    grad_inputs = (grad_middle + grad_in_norm).reshape(inputs.shape)

    gate_up_rows = jnp.stack(columns_to_rows(grad_gate_up_w))
    out_gate, out_up = merge(gate_up_rows, dp_size, ff_chunk)
    out_down = grad_down.astype(WIDE)
    grad_attn_w, out_gate, out_up, grad_inputs = tied(grad_attn_w, out_gate, out_up, grad_inputs)
    parts_qkv_w = exchanged(
        lambda rank: lax.dynamic_slice(
            grad_attn_w, (rank * gain_rows, 0), (gain_rows, qkv_width + LANES)
        )
    )
    out_query, out_key, out_value, out_out, out_gains = finish(grad_attn_w, parts_qkv_w, sharers)
    out_gains = out_gains[:, :2].T
    return (
        outputs,
        grad_inputs,
        out_gains[0],
        out_query,
        out_key,
        out_value,
        out_out,
        out_gains[1],
        out_gate,
        out_up,
        out_down,
    )


def solution(mesh):
    placed = (
        P("dp", "ctx", None, None),
        P("dp", "ctx", None),
        P(),
        P(("dp", "ctx")),
        P(("dp", "ctx"), None),
        P(("dp", "ctx"), None),
        P(("dp", "ctx"), None),
        P(("dp", "ctx"), None),
        P(("dp", "ctx")),
        P(("dp", "ctx"), None),
        P(("dp", "ctx"), None),
        P(("dp", "ctx"), None),
        P("dp", "ctx", None, None),
    )
    return jax.shard_map(
        local,
        mesh=mesh,
        in_specs=placed,
        out_specs=(
            P("dp", "ctx", None, None),
            P("dp", "ctx", None, None),
            P(("dp", "ctx")),
            P(("dp", "ctx"), None),
            P(("dp", "ctx"), None),
            P(("dp", "ctx"), None),
            P(("dp", "ctx"), None),
            P(("dp", "ctx")),
            P(("dp", "ctx"), None),
            P(("dp", "ctx"), None),
            P(("dp", "ctx"), None),
        ),
        check_vma=False,
    )
```

```python
import functools

import jax
import jax.numpy as jnp
from jax import lax
from jax.experimental import pallas as pl
from jax.experimental.pallas import tpu as pltpu
from jax.sharding import PartitionSpec as P

HEADS = 32
KV_HEADS = 4
HEAD_DIM = 64
LANES = 2 * HEAD_DIM


NORM_EPS = 1e-05
ROPE_BASE = 10000.0
MASKED_SCORE = -1e30
LOW = jnp.bfloat16
WIDE = jnp.float32


def multiply(left, right):
    return jnp.dot(left, right, preferred_element_type=WIDE)


def against(left, right):
    return lax.dot_general(left, right, (((1,), (1,)), ((), ())), preferred_element_type=WIDE)


def outer_sum(left, right):
    return lax.dot_general(left, right, (((0,), (0,)), ((), ())), preferred_element_type=WIDE)


def swapped(block, distance, axis="ctx"):
    route = [(i, i ^ distance) for i in range(lax.axis_size(axis))]
    return lax.ppermute(block, axis, route)


def tied(*values):
    return lax.optimization_barrier(values)


def tied_lists(received, others):
    values = tied(*received, *others)
    return list(values[: len(received)]), list(values[len(received) :])


def ctx_gather(block, first=(), second=()):
    size = lax.axis_size("ctx")
    if size != 4:
        got = [swapped(block, k) for k in range(1, size)]
        second = second(*first) if callable(second) else second
        got, others = tied_lists(got, [*first, *second])
        return [block] + got, others
    top, low = split_rows(block, 2)
    near = [swapped(top, 1), swapped(low, 2)]
    late = [swapped(low, 1), swapped(top, 2)]
    near, first = tied_lists(near, first)
    far = [swapped(near[0], 2), swapped(near[1], 1)]
    second = second(*first) if callable(second) else second
    got, second = tied_lists(late + far, second)
    return [block, near[0], *got[:2], near[1], *got[2:]], first + second


def gather_start(block):
    if lax.axis_size("ctx") != 4:
        return []
    top, low = split_rows(block, 2)
    return [swapped(top, 1), swapped(low, 2)]


def gather_rest(block, near):
    size = lax.axis_size("ctx")
    if size != 4:
        return [swapped(block, k) for k in range(1, size)]
    top, low = split_rows(block, 2)
    return [swapped(near[0], 2), swapped(near[1], 1), swapped(low, 1), swapped(top, 2)]


def gather_end(block, near, rest):
    if lax.axis_size("ctx") != 4:
        return [block, *rest]
    return [block, near[0], rest[2], rest[3], near[1], rest[0], rest[1]]


def ctx_scatter_sum(values, first=(), second=()):
    size = lax.axis_size("ctx")
    parts = split_rows(values, size)
    if size != 4:
        got = [swapped(parts[k].astype(LOW), k) for k in range(1, size)]
        got, others = tied_lists(got, [*first, *second])
        return sum([part.astype(WIDE) for part in got], parts[0].astype(WIDE)), others
    half = parts[0].shape[-1] // 2
    left = [part[:, :half] for part in parts]
    right = [part[:, half:] for part in parts]
    got = [
        swapped(jnp.stack([left[1], left[3]]).astype(LOW), 1),
        swapped(jnp.stack([right[2], right[3]]).astype(LOW), 2),
    ]
    (got_left, got_right), first = tied_lists(got, first)
    got_left, got_right = got_left.astype(WIDE), got_right.astype(WIDE)
    got = [
        swapped((left[2].astype(WIDE) + got_left[1]).astype(LOW), 2),
        swapped((right[1].astype(WIDE) + got_right[1]).astype(LOW), 1),
    ]
    (far_left, far_right), second = tied_lists(got, second)
    total = jnp.concatenate(
        [
            left[0].astype(WIDE) + got_left[0] + far_left.astype(WIDE),
            right[0].astype(WIDE) + got_right[0] + far_right.astype(WIDE),
        ],
        -1,
    )
    return total, first + second


def in_rank_order(parts):
    me = lax.axis_index("ctx")
    stacked = jnp.stack(parts)
    return [
        lax.dynamic_index_in_dim(stacked, me ^ r, 0, keepdims=False) for r in range(len(parts))
    ]


def exchanged(pick):
    me = lax.axis_index("ctx")
    return [pick(me)] + [swapped(pick(me ^ k), k) for k in range(1, lax.axis_size("ctx"))]


def columns_to_rows(block):
    me = lax.axis_index("ctx")
    size = lax.axis_size("ctx")
    rows = block.shape[0] // size
    pieces = [lax.dynamic_slice_in_dim(block, (me ^ k) * rows, rows, 0) for k in range(size)]
    return in_rank_order([pieces[0]] + [swapped(pieces[k], k) for k in range(1, size)])


def dp_gather(block):
    return lax.all_gather(block, "dp", axis=0, tiled=True)


def dp_scatter_sum(block):
    return lax.psum_scatter(block, "dp", scatter_dimension=0, tiled=True)


def lane_of(shape):
    return lax.broadcasted_iota(jnp.int32, shape, 1)


def turned(values):
    first = lane_of(values.shape) % HEAD_DIM < HEAD_DIM // 2
    return jnp.where(
        first,
        pltpu.roll(values, LANES - HEAD_DIM // 2, 1),
        pltpu.roll(values, HEAD_DIM // 2, 1),
    )


def both_heads(pair):
    even = lane_of(pair.shape) < HEAD_DIM
    zero = jnp.zeros_like(pair)
    return jnp.concatenate([jnp.where(even, pair, zero), jnp.where(even, zero, pair)], 0)


def one_pair(stacked):
    rows = stacked.shape[0] // 2
    even = lane_of((rows, LANES)) < HEAD_DIM
    return jnp.where(even, stacked[:rows], stacked[rows:])


def seen(rows, chunk, last_key):
    query = lax.broadcasted_iota(jnp.int32, (rows, chunk), 0) % (chunk // 2)
    key = lax.broadcasted_iota(jnp.int32, (rows, chunk), 1)
    return key <= query + last_key


def attend_kernel(pairs, chunk, order, q_ref, kv_ref, cos_ref, sin_ref, cosb_ref, sinb_ref,
                  out_ref, rot_ref, keys_ref, values_ref, lse_ref):
    rows = chunk // 2
    step = pl.program_id(0)
    chunks = keys_ref.shape[0] // chunk

    @pl.when(step == 0)
    def _():
        for b in range(keys_ref.shape[0] // rows):
            here = slice(b * rows, (b + 1) * rows)
            there = pl.ds(pl.multiple_of(order[b] * rows, rows), rows)
            own = kv_ref[here, :]
            other = pltpu.roll(own, HEAD_DIM, 1)
            low = lane_of(own.shape) < HEAD_DIM
            keys = jnp.where(low, own, other)
            keys = keys * cos_ref[here, :] + turned(keys) * sin_ref[here, :]
            keys_ref[there, :] = keys.astype(LOW)
            values_ref[there, :] = jnp.where(low, other, own).astype(LOW)

    cosine, sine = cosb_ref[...], sinb_ref[...]
    place = order[step]
    last_key = (place % 2) * rows
    for p in range(pairs):
        lanes = slice(p * LANES, (p + 1) * LANES)
        pair = q_ref[:, lanes]
        pair = pair * cosine + turned(pair) * sine
        rot_ref[:, lanes] = (pair.astype(LOW).astype(WIDE) * HEAD_DIM**-0.5).astype(LOW)

    for count in range(1, chunks + 1):

        @pl.when(place // 2 == count - 1)
        def _(count=count):
            visible = seen(2 * rows, chunk, last_key)
            all_lse = jnp.zeros((rows, LANES), WIDE)
            lane = lane_of((rows, LANES))
            for p in range(pairs):
                lanes = slice(p * LANES, (p + 1) * LANES)
                queries = both_heads(rot_ref[:, lanes])
                scores = [
                    against(queries, keys_ref[c * chunk : (c + 1) * chunk, :]) for c in range(count)
                ]
                scores[-1] = jnp.where(visible, scores[-1], MASKED_SCORE)
                top = jnp.max(functools.reduce(jnp.maximum, scores), 1, keepdims=True)
                weights = [jnp.exp(s - top) for s in scores]
                total = jnp.sum(functools.reduce(jnp.add, weights), 1, keepdims=True)
                mixture = sum(
                    multiply(w.astype(LOW), values_ref[c * chunk : (c + 1) * chunk, :])
                    for c, w in enumerate(weights)
                )
                out_ref[:, lanes] = one_pair(mixture / total).astype(LOW)
                lse = top + jnp.log(total)
                all_lse = jnp.where(lane == 2 * p, lse[:rows], all_lse)
                all_lse = jnp.where(lane == 2 * p + 1, lse[rows:], all_lse)
            lse_ref[...] = all_lse


def attend_back_kernel(pairs, chunk, order, rot_ref, grad_ref, out_ref, lse_ref, cosb_ref, sinb_ref,
                       keys_ref, values_ref, cos_ref, sin_ref, dqkv_ref, dkeys, dvalues, flat):
    rows = chunk // 2
    step = pl.program_id(0)
    steps = pl.num_programs(0)
    chunks = keys_ref.shape[0] // chunk
    scale = HEAD_DIM**-0.5

    @pl.when(step == 0)
    def _():
        dkeys[...] = jnp.zeros_like(dkeys)
        dvalues[...] = jnp.zeros_like(dvalues)

    place = order[step]
    last_chunk = place // 2
    last_key = (place % 2) * rows
    here = pl.ds(pl.multiple_of(step * rows, rows), rows)
    queries, grads, lses, deltas = [], [], [], []
    for p in range(pairs):
        lanes = slice(p * LANES, (p + 1) * LANES)
        queries.append(both_heads(rot_ref[:, lanes]))
        grads.append(both_heads(grad_ref[:, lanes]))
        product = grad_ref[:, lanes].astype(WIDE) * out_ref[:, lanes].astype(WIDE)
        low = lane_of(product.shape) < HEAD_DIM
        deltas.append(
            jnp.concatenate(
                [
                    jnp.sum(jnp.where(low, product, 0.0), 1, keepdims=True),
                    jnp.sum(jnp.where(low, 0.0, product), 1, keepdims=True),
                ],
                0,
            )
        )
        lses.append(
            jnp.concatenate(
                [lse_ref[:, 2 * p : 2 * p + 1], lse_ref[:, 2 * p + 1 : 2 * p + 2]], 0
            )
        )
    queries_t = [q.T for q in queries]
    grads_t = [g.T for g in grads]

    cosine, sine = cosb_ref[...], sinb_ref[...]
    for count in range(1, chunks + 1):

        @pl.when(last_chunk == count - 1)
        def _(count=count):
            visible = seen(2 * rows, chunk, last_key)
            for p in range(pairs):
                dq = None
                for c in range(count):
                    place_c = slice(c * chunk, (c + 1) * chunk)
                    keys = keys_ref[place_c, :]
                    values = values_ref[place_c, :]
                    weights = jnp.exp(against(queries[p], keys) - lses[p])
                    if c == count - 1:
                        weights = jnp.where(visible, weights, 0.0)
                    slopes = against(grads[p], values)
                    ds = (weights * (slopes - deltas[p])).astype(LOW)
                    part = multiply(ds, keys)
                    dq = part if dq is None else dq + part
                    dkeys[c] += multiply(queries_t[p], ds)
                    dvalues[c] += multiply(grads_t[p], weights.astype(LOW))
                pair = one_pair(dq) * scale
                pair = pair * cosine - turned(pair) * sine
                dqkv_ref[here, p * LANES : (p + 1) * LANES] = pair.astype(LOW)

    @pl.when(step == steps - 1)
    def _():
        for c in range(chunks):
            dk, dv = dkeys[c], dvalues[c]
            side = jnp.concatenate(
                [dk[:HEAD_DIM] + dk[HEAD_DIM:], dv[:HEAD_DIM] + dv[HEAD_DIM:]], 0
            )
            flat[c * chunk : (c + 1) * chunk, :] = side.T
        for b in range(keys_ref.shape[0] // rows):
            mine = slice(b * rows, (b + 1) * rows)
            there = pl.ds(pl.multiple_of(order[b] * rows, rows), rows)
            own = flat[there, :]
            back = own * cos_ref[mine, :] - turned(own) * sin_ref[mine, :]
            low = lane_of(own.shape) < HEAD_DIM
            dqkv_ref[mine, pairs * LANES :] = jnp.where(low, back, own).astype(LOW)


def attend(order, qkv, cosine, sine, rows):
    seq, width = qkv.shape[0], qkv.shape[1] - LANES
    pairs = width // LANES
    blocks = seq // rows
    block = lambda w: pl.BlockSpec((rows, w), lambda i, _: (i, 0))
    whole = lambda w, at=0: pl.BlockSpec((seq, w), lambda i, _: (0, at))
    return pl.pallas_call(
        functools.partial(attend_kernel, pairs, 2 * rows),
        grid_spec=pltpu.PrefetchScalarGridSpec(
            num_scalar_prefetch=1,
            grid=(blocks,),
            in_specs=[block(width), whole(LANES, pairs), whole(LANES), whole(LANES), block(LANES), block(LANES)],
            out_specs=[block(width), block(width), whole(LANES), whole(LANES), block(LANES)],
        ),
        out_shape=[
            jax.ShapeDtypeStruct((seq, width), LOW),
            jax.ShapeDtypeStruct((seq, width), LOW),
            jax.ShapeDtypeStruct((seq, LANES), LOW),
            jax.ShapeDtypeStruct((seq, LANES), LOW),
            jax.ShapeDtypeStruct((seq, LANES), WIDE),
        ],
        compiler_params=pltpu.CompilerParams(vmem_limit_bytes=60 << 20),
        cost_estimate=pl.CostEstimate(flops=2 * 2 * seq * seq * width, bytes_accessed=8 << 20, transcendentals=seq * seq * width // HEAD_DIM // 2),
        name="attend",
    )(order, qkv, qkv, cosine, sine, cosine, sine)


def attend_back(order, rotated, grad, out, lse, keys, values, cosine, sine, rows):
    seq, width = rotated.shape
    pairs = width // LANES
    blocks = seq // rows
    block = lambda w: pl.BlockSpec((rows, w), lambda i, _: (i, 0))
    whole = lambda w: pl.BlockSpec((seq, w), lambda i, _: (0, 0))
    chunks = seq // (2 * rows)
    return pl.pallas_call(
        functools.partial(attend_back_kernel, pairs, 2 * rows),
        grid_spec=pltpu.PrefetchScalarGridSpec(
            num_scalar_prefetch=1,
            grid=(blocks,),
            in_specs=[block(width), block(width), block(width), block(LANES), block(LANES), block(LANES),
                      whole(LANES), whole(LANES), whole(LANES), whole(LANES)],
            out_specs=whole(width + LANES),
            scratch_shapes=[
                pltpu.VMEM((chunks, LANES, 2 * rows), WIDE),
                pltpu.VMEM((chunks, LANES, 2 * rows), WIDE),
                pltpu.VMEM((seq, LANES), WIDE),
            ],
        ),
        out_shape=jax.ShapeDtypeStruct((seq, width + LANES), LOW),
        compiler_params=pltpu.CompilerParams(vmem_limit_bytes=48 << 20),
        cost_estimate=pl.CostEstimate(flops=5 * 2 * seq * seq * width, bytes_accessed=8 << 20, transcendentals=seq * seq * width // HEAD_DIM // 2),
        name="attend_back",
    )(order, rotated, grad, out, lse, cosine, sine, keys, values, cosine, sine)


def attn_sums_kernel(count, me_ref, hidden_ref, grad_ref, weight_ref, slopes_ref, *refs):
    *out_refs, joined_ref = refs
    outer, chunk = count // len(out_refs), joined_ref.shape[0] // count
    rows = out_refs[0].shape[0] // outer
    cuts = chunk // rows
    cut = out_refs[0].shape[1] // cuts
    width = grad_ref.shape[1]
    for k, ref in enumerate(out_refs):
        for i in range(outer):
            block = (me_ref[0] ^ k) * outer + i
            for j in range(cuts):
                there = pl.ds(pl.multiple_of(block * chunk, chunk) + j * rows, rows)
                joined_ref[there, width + LANES :] = ref[
                    i * rows : (i + 1) * rows, j * cut : (j + 1) * cut
                ]
    grad = grad_ref[...]
    lane = lane_of((chunk, LANES))
    for d in range(count):
        here = slice(d * chunk, (d + 1) * chunk)
        sums = lax.dot_general(
            hidden_ref[:, here], grad, (((0,), (0,)), ((), ())), preferred_element_type=WIDE
        )
        joined_ref[here, :width] = sums.astype(LOW)
        gain = weight_ref[here, width:].astype(WIDE)[:, :1]
        slope = jnp.sum(sums * weight_ref[here, :width].astype(WIDE), 1, keepdims=True) / gain
        both = jnp.where(lane == 0, slope, slopes_ref[here, :])
        joined_ref[here, width : width + LANES] = both.astype(LOW)


def attn_sums(hidden, grad, weight, slopes, parts, count):
    depth, width = hidden.shape[1], grad.shape[1]
    total = sum(part.shape[0] for part in parts)
    full = width + LANES + parts[0].shape[1] * total // depth
    vmem = pl.BlockSpec(memory_space=pltpu.VMEM)
    return pl.pallas_call(
        functools.partial(attn_sums_kernel, count),
        in_specs=[pl.BlockSpec(memory_space=pltpu.SMEM)] + [vmem] * (4 + len(parts)),
        out_specs=vmem,
        out_shape=jax.ShapeDtypeStruct((depth, full), LOW),
        compiler_params=pltpu.CompilerParams(vmem_limit_bytes=48 << 20),
        cost_estimate=pl.CostEstimate(
            flops=2 * hidden.shape[0] * depth * width, bytes_accessed=16 << 20, transcendentals=0
        ),
        name="attn_sums",
    )(lax.axis_index("ctx").reshape(1), hidden, grad, weight, slopes, *parts)


def finish_kernel(sharers, me_ref, joined_ref, *refs):
    *part_refs, query_ref, key_ref, value_ref, out_ref, gains_ref = refs
    ranks = len(part_refs)
    rows, full = part_refs[0].shape
    width = full - LANES
    query_width = query_ref.shape[1] // ranks
    head_dim = (width - query_width) // 2
    for k, ref in enumerate(part_refs):
        there = pl.ds(pl.multiple_of((me_ref[0] ^ k) * query_width, query_width), query_width)
        query_ref[:, there] = ref[:, :query_width].astype(WIDE)
    rests = [ref[:, query_width:width].astype(WIDE) for ref in part_refs]
    gains_ref[...] = sum(ref[:, width:].astype(WIDE) for ref in part_refs)
    for group in range(ranks // sharers):
        total = jnp.zeros((rows, 2 * head_dim), WIDE)
        for k, rest in enumerate(rests):
            total = total + jnp.where((me_ref[0] ^ k) // sharers == group, rest, 0.0)
        here = slice(group * head_dim, (group + 1) * head_dim)
        key_ref[:, here] = total[:, :head_dim]
        value_ref[:, here] = total[:, head_dim:]
    cut = joined_ref.shape[1] - full
    for j in range(out_ref.shape[1] // cut):
        out_ref[:, j * cut : (j + 1) * cut] = joined_ref[
            j * rows : (j + 1) * rows, full:
        ].astype(WIDE)


def finish(joined, parts, sharers):
    ranks, rows = len(parts), parts[0].shape[0]
    depth = joined.shape[0] // rows * (joined.shape[1] - parts[0].shape[1])
    head_dim = HEAD_DIM
    query_width = parts[0].shape[1] - 2 * head_dim - LANES
    vmem = pl.BlockSpec(memory_space=pltpu.VMEM)
    widths = [ranks * query_width] + [ranks // sharers * head_dim] * 2 + [depth, LANES]
    return pl.pallas_call(
        functools.partial(finish_kernel, sharers),
        in_specs=[pl.BlockSpec(memory_space=pltpu.SMEM)] + [vmem] * (1 + ranks),
        out_specs=[vmem] * 5,
        out_shape=[jax.ShapeDtypeStruct((rows, width), WIDE) for width in widths],
        name="finish",
    )(lax.axis_index("ctx").reshape(1), joined, *parts)


def place_kernel(outer, me_ref, *refs):
    *part_refs, out_ref, arrived = refs
    rows = out_ref.shape[2]
    copies = [
        pltpu.make_async_copy(
            ref.at[pl.ds(i * rows, rows), :],
            out_ref.at[i, me_ref[0] ^ k],
            arrived.at[k * outer + i],
        )
        for k, ref in enumerate(part_refs)
        for i in range(outer)
    ]
    for copy in copies:
        copy.start()
    for copy in copies:
        copy.wait()


def placed_by_rank(parts, outer):
    rows, width = parts[0].shape[0] // outer, parts[0].shape[1]
    out = pl.pallas_call(
        functools.partial(place_kernel, outer),
        in_specs=[pl.BlockSpec(memory_space=pltpu.SMEM)]
        + [pl.BlockSpec(memory_space=pltpu.HBM)] * len(parts),
        out_specs=pl.BlockSpec(memory_space=pltpu.VMEM),
        out_shape=jax.ShapeDtypeStruct((outer, len(parts), rows, width), parts[0].dtype),
        scratch_shapes=[pltpu.SemaphoreType.DMA((outer * len(parts),))],
        compiler_params=pltpu.CompilerParams(vmem_limit_bytes=40 << 20),
        name="place",
    )(lax.axis_index("ctx").reshape(1), *parts)
    return out.reshape(-1, width)


def spread_kernel(dp_size, chunk, gate_ref, up_ref, out_ref):
    ranks, _, width = out_ref.shape
    for side, ref in enumerate((gate_ref, up_ref)):
        for r in range(ranks):
            for d in range(dp_size):
                here = side * width // 2 + d * chunk
                there = (d * ranks + r) * chunk
                out_ref[r, :, here : here + chunk] = ref[:, there : there + chunk]


def merge_kernel(dp_size, chunk, parts_ref, gate_ref, up_ref):
    ranks, _, width = parts_ref.shape
    for side, ref in enumerate((gate_ref, up_ref)):
        for r in range(ranks):
            for d in range(dp_size):
                here = side * width // 2 + d * chunk
                there = (d * ranks + r) * chunk
                ref[:, there : there + chunk] = parts_ref[r, :, here : here + chunk].astype(WIDE)


def spread(gate, up, dp_size, ctx_size, chunk):
    shape = (ctx_size, gate.shape[0], 2 * dp_size * chunk)
    return pl.pallas_call(
        functools.partial(spread_kernel, dp_size, chunk),
        out_shape=jax.ShapeDtypeStruct(shape, gate.dtype),
        name="spread",
    )(gate, up)


def merge(parts, dp_size, chunk):
    shape = jax.ShapeDtypeStruct((parts.shape[1], parts.shape[0] * dp_size * chunk), WIDE)
    return pl.pallas_call(
        functools.partial(merge_kernel, dp_size, chunk), out_shape=[shape, shape], name="merge"
    )(parts)


def tiles(width, size):
    return [slice(at, min(at + size, width)) for at in range(0, width, size)]


def gate_up_kernel(gate_w_ref, up_w_ref, *refs):
    *piece_refs, gate_ref, up_ref, active_ref, hidden_ref, rows, arrived, left = refs
    copy_out = pltpu.make_async_copy(rows, hidden_ref, left)

    @pl.when(pl.program_id(0) == 0)
    def _():
        copies, at = [], 0
        for k, ref in enumerate(piece_refs):
            here = pl.ds(at, ref.shape[0])
            copies.append(pltpu.make_async_copy(ref, rows.at[here, :], arrived.at[k]))
            copies[-1].start()
            at += ref.shape[0]
        for copy in copies:
            copy.wait()
        copy_out.start()

    width = gate_ref.shape[1]
    sides = jnp.concatenate([gate_w_ref[...], up_w_ref[...]], 1)
    both = multiply(rows[...], sides)
    gate, up = both[:, :width], both[:, width:]
    gate_ref[...] = gate
    up_ref[...] = up
    active_ref[...] = (gate * jax.nn.sigmoid(gate) * up).astype(LOW)

    @pl.when(pl.program_id(0) == pl.num_programs(0) - 1)
    def _():
        copy_out.wait()


def gate_up(pieces, weight):
    depth, width = weight.shape[0], weight.shape[1] // 2
    count = sum(piece.shape[0] for piece in pieces)
    if width % LANES:
        hidden = jnp.concatenate(pieces, 0)
        gate, up = multiply(hidden, weight[:, :width]), multiply(hidden, weight[:, width:])
        return gate, up, (gate * jax.nn.sigmoid(gate) * up).astype(LOW), hidden
    steps = width // LANES
    there = pl.BlockSpec(memory_space=pl.ANY)
    block = pl.BlockSpec((count, LANES), lambda j: (0, j))
    return pl.pallas_call(
        gate_up_kernel,
        grid=(steps,),
        in_specs=[
            pl.BlockSpec((depth, LANES), lambda j: (0, j)),
            pl.BlockSpec((depth, LANES), lambda j: (0, j + steps)),
        ]
        + [pl.BlockSpec(memory_space=pltpu.HBM)] * len(pieces),
        out_specs=[block, block, block, there],
        out_shape=[
            jax.ShapeDtypeStruct((count, width), WIDE),
            jax.ShapeDtypeStruct((count, width), WIDE),
            jax.ShapeDtypeStruct((count, width), LOW),
            jax.ShapeDtypeStruct((count, depth), LOW),
        ],
        scratch_shapes=[
            pltpu.VMEM((count, depth), LOW),
            pltpu.SemaphoreType.DMA((len(pieces),)),
            pltpu.SemaphoreType.DMA,
        ],
        compiler_params=pltpu.CompilerParams(vmem_limit_bytes=60 << 20),
        cost_estimate=pl.CostEstimate(
            flops=4 * count * depth * width, bytes_accessed=36 << 20, transcendentals=count * width
        ),
        name="gate_up",
    )(weight, weight, *pieces)


def down_sums_kernel(active_ref, *refs):
    *piece_refs, sums_ref, rows_ref, arrived = refs
    copies, at = [], 0
    for k, ref in enumerate(piece_refs):
        here = pl.ds(at, ref.shape[0])
        copies.append(pltpu.make_async_copy(ref, rows_ref.at[here, :], arrived.at[k]))
        copies[-1].start()
        at += ref.shape[0]
    turned_active = active_ref[...].T
    for copy in copies:
        copy.wait()
    for cut in tiles(sums_ref.shape[1], 2 * LANES):
        sums_ref[:, cut] = multiply(turned_active, rows_ref[:, cut]).astype(LOW)


def down_sums(active, pieces):
    count, width = active.shape
    depth = pieces[0].shape[1]
    vmem = pl.BlockSpec(memory_space=pltpu.VMEM)
    return pl.pallas_call(
        down_sums_kernel,
        in_specs=[vmem] + [pl.BlockSpec(memory_space=pl.ANY)] * len(pieces),
        out_specs=[vmem, vmem],
        out_shape=[
            jax.ShapeDtypeStruct((width, depth), LOW),
            jax.ShapeDtypeStruct((count, depth), LOW),
        ],
        scratch_shapes=[pltpu.SemaphoreType.DMA((len(pieces),))],
        compiler_params=pltpu.CompilerParams(vmem_limit_bytes=60 << 20),
        cost_estimate=pl.CostEstimate(
            flops=2 * count * depth * width, bytes_accessed=18 << 20, transcendentals=0
        ),
        name="down_sums",
    )(active, *pieces)


def mlp_back_kernel(
    top_ref, gate_ref, up_ref, down_ref, weight_ref, grads_ref, part_ref, down, weight, arrived
):
    width = gate_ref.shape[1]
    first = pl.program_id(0) == 0
    copy_down = pltpu.make_async_copy(down_ref, down, arrived.at[0])
    copy_weight = pltpu.make_async_copy(weight_ref, weight, arrived.at[1])

    @pl.when(first)
    def _():
        copy_down.start()
        copy_weight.start()
        copy_down.wait()

    top = top_ref[...]
    for cut in tiles(width, 2 * LANES):
        shifted = slice(width + cut.start, width + cut.stop)
        slope = against(top, down[cut, :])
        gate, up = gate_ref[:, cut], up_ref[:, cut]
        sigmoid = jax.nn.sigmoid(gate)
        swished = gate * sigmoid
        grads_ref[:, cut] = (slope * up * sigmoid * (1.0 + gate * (1.0 - sigmoid))).astype(LOW)
        grads_ref[:, shifted] = (slope * swished).astype(LOW)

    @pl.when(first)
    def _():
        copy_weight.wait()

    grads = grads_ref[...]
    for cut in tiles(part_ref.shape[1], 2 * LANES):
        part_ref[:, cut] = against(grads, weight[cut, :]).astype(LOW)


def mlp_back(top, gate, up, down, weight, rows):
    count, depth = top.shape
    width = gate.shape[1]
    block = lambda w: pl.BlockSpec((rows, w), lambda i: (i, 0))
    there = pl.BlockSpec(memory_space=pl.ANY)
    return pl.pallas_call(
        mlp_back_kernel,
        grid=(count // rows,),
        in_specs=[block(depth), block(width), block(width), there, there],
        out_specs=[block(2 * width), block(depth)],
        out_shape=[
            jax.ShapeDtypeStruct((count, 2 * width), LOW),
            jax.ShapeDtypeStruct((count, depth), LOW),
        ],
        scratch_shapes=[
            pltpu.VMEM(down.shape, LOW),
            pltpu.VMEM(weight.shape, LOW),
            pltpu.SemaphoreType.DMA((2,)),
        ],
        compiler_params=pltpu.CompilerParams(vmem_limit_bytes=60 << 20),
        cost_estimate=pl.CostEstimate(
            flops=6 * count * depth * width, bytes_accessed=40 << 20, transcendentals=count * width
        ),
        name="mlp_back",
    )(top, gate, up, down, weight)


def out_back_kernel(weight_ref, attn_ref, *refs):
    *piece_refs, grad_ref, sums_ref, rows, arrived = refs
    copies, at = [], 0
    for k, ref in enumerate(piece_refs):
        here = pl.ds(at, ref.shape[0])
        copies.append(pltpu.make_async_copy(ref, rows.at[here, :], arrived.at[k]))
        copies[-1].start()
        at += ref.shape[0]
    turned_attn = attn_ref[...].T
    for copy in copies:
        copy.wait()
    everything = rows[...]
    for cut in tiles(weight_ref.shape[0], 2 * LANES):
        grad_ref[:, cut] = against(everything, weight_ref[cut, :]).astype(LOW)
    for cut in tiles(weight_ref.shape[1], 2 * LANES):
        sums_ref[:, cut] = multiply(turned_attn, rows[:, cut]).astype(LOW)


def out_back(pieces, weight, attn):
    count, width = attn.shape
    depth = weight.shape[1]
    vmem = pl.BlockSpec(memory_space=pltpu.VMEM)
    return pl.pallas_call(
        out_back_kernel,
        in_specs=[vmem, vmem] + [pl.BlockSpec(memory_space=pltpu.HBM)] * len(pieces),
        out_specs=[vmem, vmem],
        out_shape=[
            jax.ShapeDtypeStruct((count, width), LOW),
            jax.ShapeDtypeStruct((width, depth), LOW),
        ],
        scratch_shapes=[
            pltpu.VMEM((count, depth), LOW),
            pltpu.SemaphoreType.DMA((len(pieces),)),
        ],
        compiler_params=pltpu.CompilerParams(vmem_limit_bytes=60 << 20),
        cost_estimate=pl.CostEstimate(
            flops=4 * count * depth * width, bytes_accessed=16 << 20, transcendentals=0
        ),
        name="out_back",
    )(weight, attn, *pieces)


def norm_scale(values):
    return lax.rsqrt(jnp.mean(values * values, -1, keepdims=True) + NORM_EPS)


def norm_back(grad_hidden, normed, scale_rows, gain):
    gain_grad = jnp.sum(grad_hidden * normed, 0)
    scaled = grad_hidden * gain
    return (
        gain_grad,
        scale_rows * (scaled - normed * jnp.mean(scaled * normed, -1, keepdims=True)),
    )


def join_kernel(me_ref, *refs):
    *block_refs, out_ref = refs
    count = len(block_refs) // 2
    for k in range(count):
        out_ref[me_ref[0] ^ (2 * k)] = block_refs[k][...]
        out_ref[me_ref[0] ^ (2 * k + 1)] = block_refs[count + k][...]


def dp_blocks(block):
    return [block] + [swapped(block, 2 * k, "dp") for k in range(1, lax.axis_size("dp") // 2)]


def dp_joined(blocks):
    rows, width = blocks[0].shape
    count = 2 * len(blocks)
    others = [swapped(block, 1, "dp") for block in blocks]
    vmem = pl.BlockSpec(memory_space=pltpu.VMEM)
    out = pl.pallas_call(
        join_kernel,
        in_specs=[pl.BlockSpec(memory_space=pltpu.SMEM)] + [vmem] * count,
        out_specs=vmem,
        out_shape=jax.ShapeDtypeStruct((count, rows, width), blocks[0].dtype),
        compiler_params=pltpu.CompilerParams(vmem_limit_bytes=40 << 20),
        name="join",
    )(lax.axis_index("dp").reshape(1), *blocks, *others)
    return out.reshape(count * rows, width)


def split_rows(values, count):
    rows = values.shape[0] // count
    return [values[k * rows : (k + 1) * rows] for k in range(count)]


def local(
    inputs,
    positions,
    block_order,
    norm_attn,
    w_query,
    w_key,
    w_value,
    w_out,
    norm_mlp,
    w_gate,
    w_up,
    w_down,
    cotangent,
):
    row_count = inputs.shape[2]
    model_width = inputs.shape[3]
    block_rows = row_count // 2
    dp_size, ctx_size = lax.axis_size("dp"), lax.axis_size("ctx")
    ctx_rank = lax.axis_index("ctx")
    head_dim = HEAD_DIM
    sharers = ctx_size // KV_HEADS
    query_width = HEADS // ctx_size * head_dim
    qkv_width = query_width + 2 * head_dim
    ff_width = w_gate.shape[1] // ctx_size
    ff_chunk = w_down.shape[0]

    x_low = inputs.reshape(row_count, model_width)
    grad_top = cotangent.reshape(row_count, model_width)
    gain_rows = norm_attn.shape[0]
    own_positions = positions.reshape(gain_rows, -1)
    position_width = own_positions.shape[1]
    own_extras = jnp.concatenate(
        [
            jnp.stack([norm_attn, norm_mlp], 1),
            (own_positions // LANES).astype(LOW),
            (own_positions % LANES).astype(LOW),
        ],
        1,
    )
    own_extras = jnp.pad(own_extras, ((0, 0), (0, LANES - own_extras.shape[1])))

    def pick_attn(rank):
        kv_start = rank // sharers * head_dim
        return jnp.concatenate(
            [
                lax.dynamic_slice_in_dim(w_query, rank * query_width, query_width, 1),
                lax.dynamic_slice_in_dim(w_key, kv_start, head_dim, 1),
                lax.dynamic_slice_in_dim(w_value, kv_start, head_dim, 1),
                own_extras,
            ],
            1,
        )

    cuts = model_width // query_width
    blocks_out = dp_blocks(w_out)
    parts_qkv = exchanged(pick_attn)
    parts_qkv, (x_low, columns) = tied_lists(
        parts_qkv, [x_low, spread(w_gate, w_up, dp_size, ctx_size, ff_chunk)]
    )
    block_qkv = jnp.concatenate(in_rank_order(parts_qkv), 0)
    gathered_qkv = dp_gather(block_qkv)
    parts_gate_up = exchanged(
        lambda rank: lax.dynamic_index_in_dim(columns, rank, 0, keepdims=False)
    )
    x_parts, (block_gate_up,) = ctx_gather(
        x_low, [jnp.concatenate(in_rank_order(parts_gate_up), 0)]
    )
    part_gate_up = dp_gather(block_gate_up)
    x_parts[-1], grad_top = tied(x_parts[-1], grad_top)
    near = gather_start(grad_top)
    x_all = jnp.concatenate(x_parts, 0)

    sent = block_qkv.reshape(ctx_size, gain_rows, -1)[:, :, qkv_width + 2 :].astype(WIDE)
    sent = LANES * sent[..., :position_width] + sent[..., position_width : 2 * position_width]
    sent = sent.reshape(ctx_size, row_count)
    ranks = [ctx_rank ^ k for k in range(ctx_size)]
    all_positions = jnp.concatenate(
        [lax.dynamic_index_in_dim(sent, r, 0, keepdims=False) for r in ranks]
    )
    frequency = ROPE_BASE ** (-jnp.arange(head_dim // 2, dtype=WIDE) * 2.0 / head_dim)
    angles = all_positions[:, None] * frequency[None, :]
    cosine = jnp.tile(jnp.cos(angles), (1, 4))
    sine = jnp.sin(angles)
    sine = jnp.concatenate([-sine, sine, -sine, sine], 1)
    order = jnp.concatenate([block_order[r] for r in ranks])

    x_wide = x_all.astype(WIDE)
    scale_all = norm_scale(x_wide)
    (gathered_qkv, cosine, sine, scale_all), waited = tied_lists(
        [gathered_qkv, cosine, sine, scale_all], [*blocks_out, *near]
    )
    blocks_out, near = waited[: len(blocks_out)], waited[len(blocks_out) :]
    gathered_out = dp_joined(blocks_out)
    out_rows = gathered_out.shape[0] // ctx_size
    parts_out = exchanged(
        lambda rank: lax.dynamic_slice_in_dim(gathered_out, rank * out_rows, out_rows, 0)
    )
    part_qkv = gathered_qkv[:, :qkv_width]
    gains = gathered_qkv[:, qkv_width:].astype(WIDE).T
    gain_attn, gain_mlp = gains[0], gains[1]
    normed_attn = x_wide * scale_all
    hidden_attn = (normed_attn * gain_attn).astype(LOW)
    qkv = multiply(hidden_attn, part_qkv)
    x_rows = x_low.astype(WIDE)

    attn_low, rotated, keys, values, log_total = attend(order, qkv, cosine, sine, block_rows)
    (attn_low,), parts_out = tied_lists([attn_low], parts_out)
    part_out = placed_by_rank(parts_out, dp_size // ctx_size)
    mixed, _ = ctx_scatter_sum(multiply(attn_low, part_out).astype(LOW))
    middle = x_rows + mixed
    middle, w_down = tied(middle, w_down)
    part_down = dp_gather(w_down)
    scale_mlp = norm_scale(middle)
    normed_mlp = middle * scale_mlp
    hidden_parts, _ = ctx_gather((normed_mlp * gain_mlp).astype(LOW))
    hidden_parts[2], grad_top, *near = tied(hidden_parts[2], grad_top, *near)
    rest = gather_rest(grad_top, near)
    rest, (gate_rows, up_rows, activated, hidden_mlp) = tied_lists(
        rest, gate_up(hidden_parts, part_gate_up)
    )
    top_parts = gather_end(grad_top, near, rest)
    part_down_w, top_all = down_sums(activated, top_parts)
    part_down_w, part_down = tied(part_down_w, part_down)
    grad_down = dp_scatter_sum(part_down_w)

    grad_gate_up, part_hidden_mlp = mlp_back(
        top_all, gate_rows, up_rows, part_down, part_gate_up, row_count
    )
    grad_hidden_mlp, (part_gate_up_w,) = ctx_scatter_sum(
        part_hidden_mlp, [outer_sum(hidden_mlp, grad_gate_up).astype(LOW)]
    )
    grad_gate_up_w = dp_scatter_sum(part_gate_up_w)
    gain_mlp_grad, grad_mid_norm = norm_back(grad_hidden_mlp, normed_mlp, scale_mlp, gain_mlp)
    grad_middle = grad_top.astype(WIDE) + grad_mid_norm

    branch_parts, (part_result, grad_down) = ctx_gather(
        grad_middle.astype(LOW), [multiply(activated, part_down).astype(LOW)], [grad_down]
    )
    branch_parts, (part_result,) = tied_lists(branch_parts, [part_result])
    grad_attn, part_out_w = out_back(branch_parts, part_out, attn_low)
    split_out = part_out_w.reshape(dp_size // ctx_size, ctx_size, -1, model_width)
    parts_out_w = exchanged(
        lambda rank: lax.dynamic_index_in_dim(split_out, rank, 1, False).reshape(-1, model_width)
    )
    grad_qkv = attend_back(
        order, rotated, grad_attn, attn_low, log_total, keys, values, cosine, sine, block_rows
    )
    part_result, (grad_qkv, *parts_out_w) = ctx_scatter_sum(
        part_result, [grad_qkv, *parts_out_w]
    )
    outputs = (middle + part_result).astype(LOW).reshape(inputs.shape)
    slopes = jnp.pad(gain_mlp_grad[:, None], ((0, 0), (1, LANES - 2)))
    part_attn_w = attn_sums(hidden_attn, grad_qkv, gathered_qkv, slopes, parts_out_w, dp_size)
    grad_hidden_attn, (part_attn_w, grad_gate_up_w) = ctx_scatter_sum(
        against(grad_qkv, part_qkv).astype(LOW), [part_attn_w], [grad_gate_up_w]
    )
    grad_attn_w = dp_scatter_sum(part_attn_w)
    scale_attn = norm_scale(x_rows)
    _, grad_in_norm = norm_back(grad_hidden_attn, x_rows * scale_attn, scale_attn, gain_attn)
    grad_inputs = (grad_middle + grad_in_norm).reshape(inputs.shape)

    gate_up_rows = jnp.stack(columns_to_rows(grad_gate_up_w))
    out_gate, out_up = merge(gate_up_rows, dp_size, ff_chunk)
    out_down = grad_down.astype(WIDE)
    grad_attn_w, out_gate, out_up, grad_inputs = tied(grad_attn_w, out_gate, out_up, grad_inputs)
    parts_qkv_w = exchanged(
        lambda rank: lax.dynamic_slice(
            grad_attn_w, (rank * gain_rows, 0), (gain_rows, qkv_width + LANES)
        )
    )
    out_query, out_key, out_value, out_out, out_gains = finish(grad_attn_w, parts_qkv_w, sharers)
    out_gains = out_gains[:, :2].T
    return (
        outputs,
        grad_inputs,
        out_gains[0],
        out_query,
        out_key,
        out_value,
        out_out,
        out_gains[1],
        out_gate,
        out_up,
        out_down,
    )


def solution(mesh):
    placed = (
        P("dp", "ctx", None, None),
        P("dp", "ctx", None),
        P(),
        P(("dp", "ctx")),
        P(("dp", "ctx"), None),
        P(("dp", "ctx"), None),
        P(("dp", "ctx"), None),
        P(("dp", "ctx"), None),
        P(("dp", "ctx")),
        P(("dp", "ctx"), None),
        P(("dp", "ctx"), None),
        P(("dp", "ctx"), None),
        P("dp", "ctx", None, None),
    )
    return jax.shard_map(
        local,
        mesh=mesh,
        in_specs=placed,
        out_specs=(
            P("dp", "ctx", None, None),
            P("dp", "ctx", None, None),
            P(("dp", "ctx")),
            P(("dp", "ctx"), None),
            P(("dp", "ctx"), None),
            P(("dp", "ctx"), None),
            P(("dp", "ctx"), None),
            P(("dp", "ctx")),
            P(("dp", "ctx"), None),
            P(("dp", "ctx"), None),
            P(("dp", "ctx"), None),
        ),
        check_vma=False,
    )
```
